256 devices in a mesh: sp: 32 (over z, y_hi, core), col: 8 (over y_lo, x).
Axes of the slice: x: 4, y: 4 (y_hi: 2, y_lo: 2; y = y_hi * 2 + y_lo), z: 8, core: 2. Of those that a mesh axis runs over, the one named last changes fastest.
Arguments:
- env_desc: bfloat16 [65536, 3280], P('sp', 'col'), may hold values from -6 to 6
- alpha: float32 [65536], P('sp'), may hold values from -0.0234375 to 0.0234375
- atom_desc: bfloat16 [4096, 3280], P('sp', 'col'), may hold values from -0.109375 to 0.109375
- desc_grad: bfloat16 [4096, 16, 3, 3280], P('sp', None, None, 'col'), may hold values from -0.109375 to 0.109375
- species: int32 [4096], P('sp'), may hold values from 0 to 3
- neighbors: int32 [4096, 16], P('sp'), may hold values from 0 to 383, as said below
Outputs:
- energies: float32 [4096], P('sp')
- forces: float32 [3, 4096], P(None, 'sp')
The draws below stay inside these ranges and needn't reach their ends.
Inputs may be any that keep to these rules, and one draw needn't show every extreme that they name: `neighbors`: entries lie in 0 to 383 and never name the atom itself (entry 128 + k for the atom at place k of its block); in every block the first slot of the block's first atom is 0 and that of its last atom is 383.
All inputs are finite; a program needn't handle non-finite values.
Results may differ from the reference program's by a relative error of at most 0.007.
Values may be sent and summed in bfloat16 or wider, within the bound.
A program may use at most 128 MiB of HBM per device.

```python
import jax
import jax.numpy as jnp
from jax import lax

L = 3280
A_DEV = 128
NEIGH = 16
SPARSE = 65536
ATOMS = 4096
N_SP = 32


def draw_neighbors(key, part):
    key = jax.random.fold_in(key, 7)
    offsets = jax.random.randint(key, (ATOMS, NEIGH), -A_DEV, A_DEV)
    offsets = jnp.where(offsets >= 0, offsets + 1, offsets)
    place = (jnp.arange(ATOMS) % A_DEV).astype(jnp.int32)
    entries = A_DEV + place[:, None] + offsets
    slot = jnp.arange(NEIGH)[None, :]
    entries = jnp.where((place[:, None] == A_DEV - 1) & (slot == 0), 3 * A_DEV - 1, entries)
    entries = jnp.where((place[:, None] == 0) & (slot == 0), 0, entries)
    return entries.astype(jnp.int32)


def touch_ends(array, rng, smallest, top_value):
    dims = array.shape
    spot = [jax.random.randint(jax.random.fold_in(rng, axis), (), 0, dims[axis]) for axis in range(len(dims))]
    array = array.at[tuple(spot)].set(smallest)
    longest = dims.index(max(dims))
    spot[longest] = (spot[longest] + 1) % dims[longest]
    return array.at[tuple(spot)].set(top_value)


def levels(own_key, shape, pieces, smallest, top_value):
    def one(axis_at, blocks):
        heights = jax.random.uniform(jax.random.fold_in(jax.random.fold_in(own_key, 6), axis_at), (blocks,), jnp.float32, smallest / len(pieces), top_value / len(pieces))
        return jnp.repeat(jnp.exp(heights), shape[axis_at] // blocks).reshape((-1,) + (1,) * (len(shape) - axis_at - 1))

    factor_of = one(*pieces[0])
    for cut in pieces[1:]:
        factor_of = factor_of * one(*cut)
    return factor_of


def gaussian(key, extent, deviation, reach, split=(), kind=jnp.bfloat16):
    loudness = levels(key, extent, split, -0.22, 0.18) if split else 1.0
    values = jax.random.normal(key, extent, jnp.float32) * deviation * loudness
    return jnp.minimum(jnp.maximum(values, -reach), reach).astype(kind)


def setup_inputs(seed: int = 0) -> dict:
    seeds = jax.random.split(jax.random.key(seed), 7)
    return {
        "env_desc": gaussian(seeds[0], (SPARSE, L), 1.0, 6.0, ((0, 32), (1, 8))),
        "alpha": gaussian(seeds[1], (SPARSE,), SPARSE ** -0.5, 0.0234375, ((0, 32),), jnp.float32),
        "atom_desc": gaussian(seeds[2], (ATOMS, L), L ** -0.5, 0.109375, ((0, 32), (1, 8))),
        "desc_grad": gaussian(seeds[3], (ATOMS, NEIGH, 3, L), L ** -0.5, 0.109375, ((0, 32), (3, 8))),
        "species": touch_ends(jax.random.randint(seeds[4], (ATOMS,), 0, 4), jax.random.fold_in(seeds[4], 1), 0, 3).astype(jnp.int32),
        "neighbors": draw_neighbors(jax.random.fold_in(seeds[6], 71), 0),
    }


def reference(env_desc, alpha, atom_desc, desc_grad, species, neighbors):
    weighted = (alpha[:, None] * env_desc.astype(jnp.float32)).astype(jnp.bfloat16)
    beta = jnp.dot(env_desc.T, weighted, preferred_element_type=jnp.float32)
    beta_low = beta.astype(jnp.bfloat16)
    projected = jnp.dot(atom_desc, beta_low, preferred_element_type=jnp.float32).astype(jnp.bfloat16)
    active = (species == 0).astype(jnp.float32)
    energies = active * jnp.sum(atom_desc.astype(jnp.float32) * projected.astype(jnp.float32), axis=1)

    grad_blocks = desc_grad.reshape(N_SP, A_DEV, NEIGH, 3, L)
    proj_blocks = projected.reshape(N_SP, A_DEV, L)

    def block_pairs(items):
        grads, projs = items
        return jnp.einsum("anxc,ac->anx", grads.astype(jnp.float32), projs.astype(jnp.float32))

    pairs = lax.map(block_pairs, (grad_blocks, proj_blocks)).reshape(ATOMS, NEIGH, 3)
    pairs = pairs * active[:, None, None]
    owner = (jnp.arange(ATOMS) // A_DEV).astype(jnp.int32)
    target = (owner[:, None] * A_DEV - A_DEV + neighbors.astype(jnp.int32)) % ATOMS
    spread = jax.ops.segment_sum(pairs.reshape(ATOMS * NEIGH, 3), target.reshape(-1).astype(jnp.int32), num_segments=ATOMS)
    forces = (2.0 * jnp.sum(pairs, axis=1) - 2.0 * spread).T
    return energies, forces
```

```python
import functools

import jax
import jax.numpy as jnp
from jax import lax
from jax.experimental import pallas as pl
from jax.experimental.pallas import tpu as pltpu
from jax.sharding import PartitionSpec as P

MESH = pl.DeviceIdType.MESH
BF = jnp.bfloat16
F32 = jnp.float32
BLK = 416
SUP = 896
PAN = 7
KH = 1024
WROWS = 2944
CH = 368
NSEM = 128


def kernel(
    env_ref, alpha_ref, at_ref, spec_ref, nb_ref, grad_ref,
    energy_ref, force_ref,
    epad, r0, r1, r2, r3, uw, mine, osend, orecv, rsp, rrp, rsm, rrm,
    csum, ysend, yrecv, ball, ats, grads, onehot, pin, pout, proj, pair_parts, pairs, mrow, fsend, frecv,
    gsem, ssem, rsem,
):
    sp, col = lax.axis_index("sp"), lax.axis_index("col")
    core, yh, z = sp % 2, (sp // 2) % 2, sp // 4
    x, yl = col % 4, col // 4

    def dev(dx=0, fy=0, fh=0, dz=0, fc=0):
        a = 1 - yl if fy else yl
        h = 1 - yh if fh else yh
        k = 1 - core if fc else core
        return ((((z + dz + 8) % 8) * 2 + h) * 2 + k, a * 4 + (x + dx + 4) % 4)

    names = {}

    def copy(name, src, dst, where):
        i = names.setdefault(name, len(names))
        return pltpu.make_async_remote_copy(
            src_ref=src, dst_ref=dst, send_sem=ssem.at[i], recv_sem=rsem.at[i],
            device_id=where, device_id_type=MESH,
        )

    sent = []

    def start(name, src, dst, where):
        c = copy(name, src, dst, where)
        c.start()
        sent.append(c)
        return c

    def al(v, m):
        return pl.multiple_of(v, m)

    grad_copy = pltpu.make_async_copy(grad_ref, grads, gsem)
    grad_copy.start()
    epad[400:416, :] = jnp.zeros((16, 2048), BF)
    epad[0:400, :] = env_ref[0:400, :]
    epad[400:410, :] = env_ref[400:410, :]

    peers = [dev(dx=1), dev(dx=-1), dev(dx=2), dev(fy=1), dev(dx=1, fy=1), dev(dx=-1, fy=1), dev(dx=2, fy=1)]
    peers += [dev(fc=1), dev(dz=1), dev(dz=-1), dev(fh=1), dev(fy=1, fh=1)]
    peers += [dev(dx=1, fy=1, fc=1), dev(dx=-1, fy=1, fc=1), dev(dx=2, fy=1, fc=1)]
    after, before = ((sp + 1) % 32, col), ((sp + 31) % 32, col)
    peers += [after, before]
    barrier = pltpu.get_barrier_semaphore()
    for p in peers:
        pl.semaphore_signal(barrier, inc=1, device_id=p, device_id_type=MESH)
    pl.semaphore_wait(barrier, len(peers))

    mine_k = al(yl * KH, KH)
    their_k = (1 - yl) * KH
    own_rows = pl.ds(al(yl * BLK, 16), BLK)
    oth_rows = pl.ds(al((1 - yl) * BLK, 16), BLK)

    ys = {}
    for q in (0, 2, 1, 3):
        ys[q] = start(f"y{q}", epad.at[:, pl.ds(al(their_k + q * 256, 256), 256)],
                      r0.at[own_rows, pl.ds(q * 256, 256)], dev(fy=1))
    xo_p = start("xop", epad.at[:, pl.ds(al(yl * KH, 512), 512)], r2.at[own_rows, :], dev(dx=1))
    xo_m = start("xom", epad.at[:, pl.ds(al(yl * KH + 512, 512), 512)], r1.at[own_rows, :], dev(dx=-1))

    r0[own_rows, :] = epad[:, pl.ds(mine_k, KH)]
    for r in (r0, r1, r2, r3):
        r[832:896, :] = jnp.zeros((64, r.shape[1]), BF)
    weight = alpha_ref[:, pl.ds(mine_k, KH)]
    uw[own_rows, :] = (r0[own_rows, :].astype(F32) * weight).astype(BF)
    for i in range(4):
        ats[core, i * SUP + 832 : (i + 1) * SUP, :] = jnp.zeros((64, 128), BF)
    slots = lax.broadcasted_iota(jnp.int32, (384, 128), 0)
    for n in range(16):
        onehot[:, n * 128 : (n + 1) * 128] = jnp.where(slots == nb_ref[n : n + 1, :], 1.0, 0.0).astype(BF)
    mrow[...] = jnp.zeros_like(mrow)
    pair_parts[8] = jnp.zeros((56, 128), F32)

    def wave(w, lhs_of, rhs, ks):
        for part in (1, 0):
            rows = pl.ds(al((1 - core if part else core) * BLK, 16), BLK)
            for n0, n in ((0, 256), (256, 256), (512, 256), (768, 128)):
                got = None
                for lhs_lane, rhs_lane, k in ks:
                    d = lax.dot_general(
                        lhs_of[rows, pl.ds(lhs_lane, k)], rhs[n0 : n0 + n, rhs_lane : rhs_lane + k],
                        (((1,), (1,)), ((), ())), preferred_element_type=F32,
                    )
                    got = d if got is None else got + d
                for j in range(n // 128):
                    t = n0 // 128 + j
                    panel = got[:, j * 128 : (j + 1) * 128]
                    if part:
                        osend[w, t * BLK : (t + 1) * BLK, :] = panel.astype(BF)
                    else:
                        mine[w, t * BLK : (t + 1) * BLK, :] = panel
            if part:
                start(f"core{w}", osend.at[w], orecv.at[w], dev(fc=1))

    def chunk(d):
        return pl.ds(al(((d + 8) % 8) * CH, 16), CH)

    def local(w, d):
        return mine[w, chunk(d), :] + orecv[w, chunk(d), :].astype(F32)

    def rs_send(w, s):
        if s < 4:
            v = local(w, z + 4 - s)
            if s:
                live[f"rp{w}{s-1}"].wait_recv()
                v = v + rrp[w, s - 1].astype(F32)
            rsp[w, s] = v.astype(BF)
            live[f"rp{w}{s}"] = start(f"rp{w}{s}", rsp.at[w, s], rrp.at[w, s], dev(dz=1))
        if s < 3:
            v = local(w, z - 3 + s)
            if s:
                live[f"rm{w}{s-1}"].wait_recv()
                v = v + rrm[w, s - 1].astype(F32)
            rsm[w, s] = v.astype(BF)
            live[f"rm{w}{s}"] = start(f"rm{w}{s}", rsm.at[w, s], rrm.at[w, s], dev(dz=-1))

    live = {}

    def core_done(w):
        copy(f"core{w}", osend.at[w], orecv.at[w], dev(fc=1)).wait_recv()

    def rs_end(w):
        live[f"rp{w}3"].wait_recv()
        live[f"rm{w}2"].wait_recv()
        v = local(w, z) + rrp[w, 3].astype(F32) + rrm[w, 2].astype(F32)
        csum[w] = v
        ysend[w] = v.astype(BF)
        a = copy(f"ya{w}", ysend.at[w], yrecv.at[w, 0], dev(fh=1))
        b = copy(f"yb{w}", ysend.at[w], yrecv.at[w, 1], dev(fy=1))
        c = copy(f"yc{w}", ysend.at[w], yrecv.at[w, 2], dev(fy=1, fh=1))

        @pl.when(core == yl)
        def _():
            a.start()

        @pl.when(core != yl)
        def _():
            b.start()
            c.start()

        ycopies.append((a, b, c))

    ycopies = []
    gathers = []

    def ag_start(w):
        a, b, c = ycopies[w]

        @pl.when(core == yl)
        def _():
            a.wait_recv()
            b.wait_recv()
            c.wait_recv()
            v = csum[w] + yrecv[w, 0].astype(F32) + yrecv[w, 1].astype(F32) + yrecv[w, 2].astype(F32)
            ball[w, chunk(z), :] = v.astype(BF)

        ag_step(w, 0)

    def ag_copy(w, s, sign):
        ref = ball.at[w, chunk(z - s if sign > 0 else z + s)]
        return copy(f"g{sign}{w}{s}", ref, ref, dev(dz=sign))

    def ag_recv(w, s, sign):
        ref = ball.at[w, chunk(z - 1 - s if sign > 0 else z + 1 + s)]
        return copy(f"g{sign}{w}{s}", ref, ref, dev(dz=sign))

    def ag_step(w, s):
        @pl.when(core == yl)
        def _():
            if s < 4:
                if s:
                    ag_recv(w, s - 1, 1).wait_recv()
                ag_copy(w, s, 1).start()
            if s < 3:
                if s:
                    ag_recv(w, s - 1, -1).wait_recv()
                ag_copy(w, s, -1).start()

    def ag_end(w):
        @pl.when(core == yl)
        def _():
            ag_recv(w, 3, 1).wait_recv()
            ag_recv(w, 2, -1).wait_recv()

    xp = {}
    for i, q in enumerate((0, 2, 1, 3)):
        ys[q].wait_recv()
        src = r0.at[oth_rows, pl.ds(q * 256, 256)]
        lanes = pl.ds((q % 2) * 256, 256)
        if q < 2:
            xp[q] = start(f"x{q}", src, r2.at[oth_rows, lanes], dev(dx=1))
        else:
            xp[q] = start(f"x{q}", src, r1.at[oth_rows, lanes], dev(dx=-1))
        if i == 1:
            op = al(jnp.where((x + 3) % 4 < 2, 0, 256), 256)
            om = al(jnp.where((x + 1) % 4 < 2, 0, 256), 256)
            xo_p.wait_recv()
            fo_p = start("fop", r2.at[own_rows, pl.ds(op, 256)], r3.at[own_rows, pl.ds(0, 256)], dev(dx=1))
            xo_m.wait_recv()
            fo_m = start("fom", r1.at[own_rows, pl.ds(om, 256)], r3.at[own_rows, pl.ds(256, 256)], dev(dx=-1))
    uw[oth_rows, :] = (r0[oth_rows, :].astype(F32) * weight).astype(BF)
    wave(0, uw, r0, ((0, 0, KH),))
    for q in (0, 1):
        xp[q].wait_recv()
    fp_p = start("fpp", r2.at[oth_rows, pl.ds(op, 256)], r3.at[oth_rows, pl.ds(0, 256)], dev(dx=1))
    for q in (2, 3):
        xp[q].wait_recv()
    fp_m = start("fpm", r1.at[oth_rows, pl.ds(om, 256)], r3.at[oth_rows, pl.ds(256, 256)], dev(dx=-1))
    core_done(0)
    rs_send(0, 0)
    wave(1, uw, r1, ((512, 0, 512),))
    rs_send(0, 1)
    core_done(1)
    rs_send(1, 0)
    wave(2, uw, r2, ((0, 0, 512),))
    rs_send(0, 2)
    core_done(2)
    rs_send(1, 1)
    rs_send(2, 0)
    for c in (fo_p, fo_m, fp_p, fp_m):
        c.wait_recv()
    o3 = jnp.where((x + 2) % 4 < 2, 0, 256)
    wave(3, uw, r3, ((al(o3, 256), 0, 256), (al(o3 + 512, 256), 256, 256)))

    ats[core, pl.ds(al(yl * BLK + 400, 16), 16), :] = jnp.zeros((16, 128), BF)
    ats[core, pl.ds(al(yl * BLK, 16), 400), :] = at_ref[0:400, :]
    ats[core, pl.ds(al(yl * BLK + 400, 16), 10), :] = at_ref[400:410, :]
    own_at = ats.at[core, own_rows, :]
    acopies = []
    for dx, i in ((0, 0), (1, 2), (-1, 1), (2, 3)):
        for fy in (0, 1):
            if dx or fy:
                acopies.append(start(f"a{i}{fy}", own_at, ats.at[core, pl.ds(al(i * SUP + yl * BLK, 16), BLK), :], dev(dx=dx, fy=fy)))

    rs_send(0, 3)
    core_done(3)
    rs_send(1, 2)
    rs_send(2, 1)
    rs_send(3, 0)
    rs_end(0)
    rs_send(1, 3)
    rs_send(2, 2)
    rs_send(3, 1)
    ag_start(0)
    rs_end(1)
    rs_send(2, 3)
    rs_send(3, 2)
    ag_step(0, 1)
    ag_start(1)
    rs_end(2)
    rs_send(3, 3)
    ag_step(0, 2)
    ag_step(1, 1)
    ag_start(2)
    for c in acopies:
        c.wait_recv()
    hand = copy("hand", ats.at[core], ats.at[core], dev(fc=1))

    @pl.when(core != yl)
    def _():
        hand.start()

    rs_end(3)
    ag_step(0, 3)
    ag_step(1, 2)
    ag_step(2, 1)
    ag_start(3)
    ag_end(0)
    ag_step(1, 3)
    ag_step(2, 2)
    ag_step(3, 1)
    ag_end(1)
    ag_step(2, 3)
    ag_step(3, 2)
    ag_end(2)
    ag_step(3, 3)
    ag_end(3)

    pcopies = {}
    for i, dx in ((1, 1), (2, -1), (3, 2)):
        for b in (0, 1):
            pcopies[i, b] = (i, b, dx)
    phand = copy("phand", proj.at[1 - core], proj.at[1 - core], dev(fc=1))

    def p_copy(i, same):
        dx = (0, 1, -1, 2)[i]
        rows = pl.ds(al((i - 1) * SUP + (yl if same else 1 - yl) * BLK, 16), BLK)
        where = dev(dx=dx) if same else dev(dx=dx, fy=1, fc=1)
        return copy(f"p{i}{same}", pout.at[rows, :], pin.at[(i - 1) * 2 + same], where)

    @pl.when(core == yl)
    def _():
        ats_in = copy("hand", ats.at[1 - core], ats.at[1 - core], dev(fc=1))
        ats_in.wait_recv()
        own_atoms = jnp.concatenate([ats[0, own_rows, :], ats[1, own_rows, :]], axis=1)
        for i in (3, 1, 2):
            for t in range(PAN):
                got = lax.dot_general(
                    ball[i, t * BLK : (t + 1) * BLK, :], own_atoms, (((0,), (0,)), ((), ())), preferred_element_type=F32
                )
                pout[(i - 1) * SUP + t * 128 : (i - 1) * SUP + (t + 1) * 128, :] = got.astype(BF)
            for same in (1, 0):
                p_copy(i, same).start()
        total = jnp.zeros((BLK, 256), F32)
        for i in range(4):
            for t in range(PAN):
                rows = slice(i * SUP + t * 128, i * SUP + (t + 1) * 128)
                atoms = jnp.concatenate([ats[0, rows, :], ats[1, rows, :]], axis=1)
                total = total + jnp.dot(ball[i, t * BLK : (t + 1) * BLK, :], atoms, preferred_element_type=F32)
        for i in (1, 2, 3):
            for same in (1, 0):
                p_copy(i, same).wait_recv()
                total = total + pin[(i - 1) * 2 + same].astype(F32)
        proj[0] = total[:, :128].astype(BF)
        proj[1] = total[:, 128:].astype(BF)
        phand.start()

    @pl.when(core != yl)
    def _():
        copy("phand", proj.at[core], proj.at[core], dev(fc=1)).wait_recv()

    grad_copy.wait()
    acc = [jnp.zeros((16, 128), F32) for _ in range(3)]
    energy = jnp.zeros((1, 128), F32)

    def body(step, carry):
        a0, a1, a2, e = carry
        rows = pl.ds(al(step * 16, 16), 16)
        pr = proj[core, rows, :].astype(F32)
        at = ats[core, pl.ds(al(yl * BLK + step * 16, 16), 16), :].astype(F32)
        e = e + jnp.sum(pr * at, axis=0, keepdims=True)
        out = []
        for c, a in enumerate((a0, a1, a2)):
            for r in range(16):
                a = a + grads[c, step * 16 + r].astype(F32) * pr[r : r + 1, :]
            out.append(a)
        return (*out, e)

    a0, a1, a2, energy = lax.fori_loop(0, 25, body, (*acc, energy))
    pr = proj[core, 400:416, :].astype(F32)
    at = ats[core, pl.ds(al(yl * BLK + 400, 16), 16), :].astype(F32)
    energy = energy + jnp.sum(pr * at, axis=0, keepdims=True)
    out = []
    for c, a in enumerate((a0, a1, a2)):
        for r in range(10):
            a = a + grads[c, 400 + r].astype(F32) * pr[r : r + 1, :]
        out.append(a)

    for c in range(3):
        pair_parts[8, c * 16 : (c + 1) * 16, :] = out[c]
    pair_parts[8, 48:49, :] = energy
    scopies = []
    for i, (dx, fy) in enumerate(((1, 0), (-1, 0), (2, 0), (0, 1), (1, 1), (-1, 1), (2, 1))):
        scopies.append(start(f"s{i}", pair_parts.at[8], pair_parts.at[col], dev(dx=dx, fy=fy)))
    pair_parts[col] = pair_parts[8]
    for c in scopies:
        c.wait_recv()
    summed = pair_parts[0]
    for i in range(1, 8):
        summed = summed + pair_parts[i]
    active = jnp.where(spec_ref[...] == 0, 1.0, 0.0)
    energy_ref[...] = summed[48:49, :] * active
    for c in range(3):
        pairs[c] = summed[c * 16 : (c + 1) * 16, :] * active
    own = jnp.sum(pairs[...], axis=1)
    for n in range(16):
        mrow[0:3, n * 128 : (n + 1) * 128] = pairs[:, n, :]
    high = mrow[...].astype(BF)
    low = (mrow[...] - high.astype(F32)).astype(BF)
    dims = (((1,), (1,)), ((), ()))
    spread = lax.dot_general(high, onehot[...], dims, preferred_element_type=F32)
    spread = spread + lax.dot_general(low, onehot[...], dims, preferred_element_type=F32)
    fsend[0] = spread[:, 0:128]
    fsend[1] = spread[:, 256:384]
    fb = start("fb", fsend.at[0], frecv.at[0], before)
    fa = start("fa", fsend.at[1], frecv.at[1], after)
    center = 2.0 * own - 2.0 * spread[0:3, 128:256]
    fb.wait_recv()
    fa.wait_recv()
    force_ref[...] = center - 2.0 * frecv[0, 0:3, :] - 2.0 * frecv[1, 0:3, :]

    for c in sent:
        c.wait_send()

    @pl.when(core == yl)
    def _():
        for w in range(4):
            ycopies[w][0].wait_send()
            for s in range(4):
                ag_copy(w, s, 1).wait_send()
            for s in range(3):
                ag_copy(w, s, -1).wait_send()
        for i in (1, 2, 3):
            for same in (1, 0):
                p_copy(i, same).wait_send()
        phand.wait_send()

    @pl.when(core != yl)
    def _():
        for w in range(4):
            ycopies[w][1].wait_send()
            ycopies[w][2].wait_send()
        hand.wait_send()


def shards(env_desc, alpha, atom_desc, desc_grad, species, neighbors):
    vm = pl.BlockSpec(memory_space=pltpu.VMEM)
    V = pltpu.VMEM
    energies, forces = pl.pallas_call(
        kernel,
        out_shape=(jax.ShapeDtypeStruct((1, 128), F32), jax.ShapeDtypeStruct((3, 128), F32)),
        in_specs=[vm, vm, vm, vm, vm, pl.BlockSpec(memory_space=pl.ANY)],
        out_specs=(vm, vm),
        scratch_shapes=[
            V((BLK, 2048), BF),
            V((SUP, KH), BF), V((SUP, 512), BF), V((SUP, 512), BF), V((SUP, 512), BF),
            V((2 * BLK, KH), BF),
            V((4, WROWS, 128), F32), V((4, WROWS, 128), BF), V((4, WROWS, 128), BF),
            V((4, 4, CH, 128), BF), V((4, 4, CH, 128), BF), V((4, 3, CH, 128), BF), V((4, 3, CH, 128), BF),
            V((4, CH, 128), F32), V((4, CH, 128), BF), V((4, 3, CH, 128), BF),
            V((4, WROWS, 128), BF),
            V((2, 4 * SUP, 128), BF),
            V((3, 410, 16, 128), BF),
            V((384, 2048), BF),
            V((6, BLK, 256), BF), V((3 * SUP, 256), BF), V((2, BLK, 128), BF),
            V((9, 56, 128), F32), V((3, 16, 128), F32), V((8, 2048), F32),
            V((2, 8, 128), F32), V((2, 8, 128), F32),
            pltpu.SemaphoreType.DMA, pltpu.SemaphoreType.DMA((NSEM,)), pltpu.SemaphoreType.DMA((NSEM,)),
        ],
        compiler_params=pltpu.CompilerParams(
            collective_id=0, has_side_effects=True, vmem_limit_bytes=58 * 2**20
        ),
    )(
        env_desc.T,
        alpha[None, :],
        atom_desc.T,
        species[None, :],
        neighbors.T,
        jnp.transpose(desc_grad, (2, 3, 1, 0)),
    )
    return energies.reshape(128), forces


def solution(mesh):
    placed = (
        P("sp", "col"),
        P("sp"),
        P("sp", "col"),
        P("sp", None, None, "col"),
        P("sp"),
        P("sp", None),
    )
    return jax.shard_map(
        shards, mesh=mesh, in_specs=placed, out_specs=(P("sp"), P(None, "sp")), check_vma=False
    )
```

```python
import functools

import jax
import jax.numpy as jnp
from jax import lax
from jax.experimental import pallas as pl
from jax.experimental.pallas import tpu as pltpu
from jax.sharding import PartitionSpec as P

MESH = pl.DeviceIdType.MESH
BF = jnp.bfloat16
F32 = jnp.float32
BLK = 416
KC = 512
CHS = (160, 160, 208)
OFF = (0, 1280, 2560)
ROWS = 4224
PANELS = ((0, 1, 2), (3, 4, 5), (6, 7, 8, 9))
STK = 1696
NSEM = 96
NT = (((1,), (1,)), ((), ()))
TN = (((0,), (0,)), ((), ()))


def kernel(
    env_ref, alpha_ref, at_ref, spec_ref, nb_ref, grad_ref,
    out_ref,
    env, r1, r2, relay, part, uw, acc, osend, orecv, rsp, rrp, rsm, rrm, csum, ysend, yrecv, ball,
    ats, astack, arow, grads, onehot, prow, pcol, psend, precv, mout, mrecv, proj, pair_parts, pairs, mrow, fsend, frecv,
    lsem, ssem, rsem,
):
    sp, col = lax.axis_index("sp"), lax.axis_index("col")
    core, yh, z = sp % 2, (sp // 2) % 2, sp // 4
    x, yl = col % 4, col // 4

    def dev(dx=0, fy=0, fh=0, dz=0, fc=0):
        a = 1 - yl if fy else yl
        h = 1 - yh if fh else yh
        k = 1 - core if fc else core
        return ((((z + dz + 8) % 8) * 2 + h) * 2 + k, a * 4 + (x + dx + 4) % 4)

    names = {}
    sent = []

    def copy(name, src, dst, where):
        i = names.setdefault(name, len(names))
        return pltpu.make_async_remote_copy(
            src_ref=src, dst_ref=dst, send_sem=ssem.at[i], recv_sem=rsem.at[i],
            device_id=where, device_id_type=MESH,
        )

    def start(name, src, dst, where):
        c = copy(name, src, dst, where)
        c.start()
        sent.append(c)
        return c

    def al(v, m):
        return pl.multiple_of(v, m)

    env_copy = pltpu.make_async_copy(env_ref, env, lsem.at[0])
    env_copy.start()
    peers = [dev(dx=1), dev(dx=-1), dev(dx=2), dev(fy=1), dev(dx=1, fy=1), dev(dx=-1, fy=1), dev(dx=2, fy=1)]
    peers += [dev(fc=1), dev(fh=1), dev(dz=1), dev(dz=-1)]
    after, before = ((sp + 1) % 32, col), ((sp + 31) % 32, col)
    peers += [after, before]
    barrier = pltpu.get_barrier_semaphore()
    for p in peers:
        pl.semaphore_signal(barrier, inc=1, device_id=p, device_id_type=MESH)
    env_copy.wait()
    grad_copy = pltpu.make_async_copy(grad_ref, grads, lsem.at[1])
    grad_copy.start()
    r1[400:416, :] = jnp.zeros((16, 2048), BF)
    r1[0:400, :] = env[0:400, :]
    r1[400:410, :] = env[400:410, :]
    pl.semaphore_wait(barrier, len(peers))

    def order(at_x):
        t = jnp.where(at_x % 4 >= 2, 0, 1024)
        return [al(o, KC) for o in (t, t + KC, 1024 - t, 1024 - t + KC)]

    ks = order(x)
    ks_left = order(x + 3)
    first = jnp.where(x < 2, 0, 1024)
    own = slice(0, BLK)
    ys, ns, os = [], [], []
    for i in range(4):
        ys.append(start(f"y{i}", r1.at[own, pl.ds(ks[i], KC)], part.at[:, pl.ds(ks[i], KC)], dev(fy=1)))
        ns.append(start(f"n{i}", r1.at[own, pl.ds(ks_left[i], KC)], r1.at[BLK : 2 * BLK, pl.ds(ks_left[i], KC)], dev(dx=-1)))
        os.append(start(f"o{i}", r1.at[own, pl.ds(al(first + i * 256, 256), 256)], relay.at[:, pl.ds(i * 256, 256)], dev(dx=1)))

    def n_wait(i):
        copy(f"n{i}", r1.at[own, pl.ds(ks[i], KC)], r1.at[BLK : 2 * BLK, pl.ds(ks[i], KC)], dev(dx=-1)).wait_recv()

    rs = []

    def pass_on(i):
        os[i].wait_recv()
        rs.append(start(f"r{i}", relay.at[:, pl.ds(i * 256, 256)], r2.at[64 : 64 + BLK, pl.ds(i * 256, 256)], dev(dx=1)))

    r1[832:896, :] = jnp.zeros((64, 2048), BF)
    r2[0:64, :] = jnp.zeros((64, 1024), BF)
    r2[480:512, :] = jnp.zeros((32, 1024), BF)
    uw[0] = (r1[own, :].astype(F32) * alpha_ref[...]).astype(BF)
    slots = lax.broadcasted_iota(jnp.int32, (384, 128), 0)
    for n in range(16):
        onehot[:, n * 128 : (n + 1) * 128] = jnp.where(slots == nb_ref[n : n + 1, :], 1.0, 0.0).astype(BF)
    mrow[...] = jnp.zeros_like(mrow)
    pair_parts[8] = jnp.zeros((56, 128), F32)
    ats[core, 1248:1280, :] = jnp.zeros((32, 128), BF)
    ats[core, 400:416, :] = jnp.zeros((16, 128), BF)
    ats[core, 0:400, :] = at_ref[0:400, :]
    ats[core, 400:410, :] = at_ref[400:410, :]

    def spot(t):
        g = 0 if t < 3 else 1 if t < 6 else 2
        return OFF[g] + (t - PANELS[g][0]) * BLK

    def product(b, k, rhs, r0, n, rk):
        return lax.dot_general(
            uw[b, :, pl.ds(k, KC)], rhs[r0 : r0 + n, pl.ds(rk, KC)], NT, preferred_element_type=F32
        )

    def add(b, t, v, fresh):
        at = slice(spot(t), spot(t) + BLK)
        acc[b, at, :] = v if fresh else acc[b, at, :] + v

    def step(i):
        ys[i].wait_recv()
        n_wait(i)
        k = ks[i]
        uw[1, :, pl.ds(k, KC)] = (part[:, pl.ds(k, KC)].astype(F32) * alpha_ref[:, pl.ds(k, KC)]).astype(BF)
        if i == 3:
            return
        for b in (0, 1):
            for r0, n in ((0, 256), (256, 256), (512, 256), (768, 128)):
                v = product(b, k, r1, r0, n, k)
                for j in range(n // 128):
                    add(b, r0 // 128 + j, v[:, j * 128 : (j + 1) * 128], i == 0)

    def opposite():
        rs[0].wait_recv()
        rs[1].wait_recv()
        for b in (0, 1):
            for r0, n in ((0, 128), (128, 256), (384, 128)):
                v = product(b, ks[0], r2, r0, n, 0)
                for j in range(n // 128):
                    t = 6 + r0 // 128 + j
                    add(b, t, v[:, j * 128 : (j + 1) * 128], t > 6)

    def last(g):
        for other in (1, 0):
            b = 1 - core if other else core
            if g < 2:
                parts = [(PANELS[g][0], ((r1, 3, g * 384, 256, 0),)), (PANELS[g][2], ((r1, 3, g * 384 + 256, 128, 0),))]
            else:
                parts = [
                    (6, ((r1, 3, 768, 128, 0), (r2, 1, 0, 128, 1))),
                    (7, ((r2, 1, 128, 256, 1),)),
                    (9, ((r2, 1, 384, 128, 1),)),
                ]
            for t0, terms in parts:
                v = None
                for rhs, i, r0, n, compact in terms:
                    d = product(b, ks[i], rhs, r0, n, KC if compact else ks[i])
                    v = d if v is None else v + d
                for j in range(n // 128):
                    at = slice(spot(t0 + j), spot(t0 + j) + BLK)
                    full = acc[b, at, :] + v[:, j * 128 : (j + 1) * 128]
                    if other:
                        osend[at, :] = full.astype(BF)
                    else:
                        acc[b, at, :] = full
            if other:
                rows = slice(OFF[g], OFF[g] + 8 * CHS[g])
                cores.append(start(f"core{g}", osend.at[rows, :], orecv.at[rows, :], dev(fc=1)))

    cores = []

    def chunk(g, d):
        return pl.ds(al(OFF[g] + ((d + 8) % 8) * CHS[g], 16), CHS[g])

    def slot(g):
        return slice(OFF[g] // 8, OFF[g] // 8 + CHS[g])

    def local(g, d):
        return acc[core, chunk(g, d), :] + orecv[chunk(g, d), :].astype(F32)

    live = {}

    def ring(g, far):
        return (1 if far == 4 else -1) * (1 if g % 2 == 0 else -1)

    def rs_send(g, s):
        if s == 0:
            cores[g].wait_recv()
        for far, sbuf, rbuf in ((4, rsp, rrp), (3, rsm, rrm)):
            if s >= far:
                continue
            way = ring(g, far)
            v = local(g, z + way * (far - s))
            if s:
                live[g, far, s - 1].wait_recv()
                v = v + rbuf[s - 1, slot(g), :].astype(F32)
            sbuf[s, slot(g), :] = v.astype(BF)
            live[g, far, s] = start(f"s{far}{g}{s}", sbuf.at[s, slot(g), :], rbuf.at[s, slot(g), :], dev(dz=way))

    ycopies = {}

    def rs_end(g):
        live[g, 4, 3].wait_recv()
        live[g, 3, 2].wait_recv()
        v = local(g, z) + rrp[3, slot(g), :].astype(F32) + rrm[2, slot(g), :].astype(F32)
        csum[slot(g), :] = v
        ysend[slot(g), :] = v.astype(BF)
        ycopies[g] = start(f"h{g}", ysend.at[slot(g), :], yrecv.at[slot(g), :], dev(fh=1))

    def ag_start(g):
        ycopies[g].wait_recv()
        ball[chunk(g, z), :] = (csum[slot(g), :] + yrecv[slot(g), :].astype(F32)).astype(BF)
        ag_step(g, 0)

    def ag_copy(g, s, far, recv=0):
        ref = ball.at[chunk(g, z - ring(g, far) * (s + recv)), :]
        return copy(f"g{far}{g}{s}", ref, ref, dev(dz=ring(g, far)))

    def ag_step(g, s):
        for far in (4, 3):
            if s < far:
                if s:
                    ag_copy(g, s - 1, far, 1).wait_recv()
                c = ag_copy(g, s, far)
                c.start()
                sent.append(c)

    def ag_end(g):
        for far in (4, 3):
            ag_copy(g, far - 1, far, 1).wait_recv()

    pass_on(0)
    pass_on(1)
    step(0)
    pass_on(2)
    pass_on(3)
    step(1)
    step(2)
    opposite()
    step(3)
    last(0)
    last(1)
    rs_send(0, 0)
    rs[2].wait_recv()
    rs[3].wait_recv()
    last(2)
    rs_send(1, 0)
    rs_send(2, 0)
    own_at = ats.at[core, own, :]
    acopies = [
        start("an", own_at, ats.at[core, BLK : 2 * BLK, :], dev(dx=-1)),
        start("ao", own_at, ats.at[core, 2 * BLK : 3 * BLK, :], dev(dx=2)),
        start("ap", own_at, ats.at[core, 1280:STK, :], dev(fy=1)),
    ]
    rs_send(0, 1)
    rs_send(1, 1)
    rs_send(2, 1)
    rs_send(0, 2)
    rs_send(1, 2)
    rs_send(2, 2)
    for c in acopies:
        c.wait_recv()
    hand = start("hand", ats.at[core], ats.at[core], dev(fc=1))
    rs_send(0, 3)
    rs_send(1, 3)
    rs_end(0)
    rs_send(2, 3)
    rs_end(1)
    rs_end(2)
    copy("hand", ats.at[1 - core], ats.at[1 - core], dev(fc=1)).wait_recv()
    both = jnp.concatenate([ats[0], ats[1]], axis=1)
    astack[...] = both[0:1280, :]

    @pl.when(core == 0)
    def _():
        arow[...] = both[0:BLK, :]

    @pl.when(core == 1)
    def _():
        arow[...] = both[1280:STK, :]
        astack[0:BLK, :] = jnp.zeros((BLK, 256), BF)

    ag_start(0)
    ag_start(1)
    ag_start(2)
    ag_step(0, 1)
    ag_step(1, 1)
    ag_step(2, 1)
    ag_step(0, 2)
    ag_step(1, 2)
    ag_step(2, 2)
    ag_step(0, 3)
    ag_step(1, 3)

    def p_terms(g):
        total = None
        for t in PANELS[g]:
            beta = ball[spot(t) : spot(t) + BLK, :]
            pcol[t * 128 : (t + 1) * 128, :] = lax.dot_general(beta, arow[...], TN, preferred_element_type=F32)
            d = jnp.dot(beta, astack[t * 128 : (t + 1) * 128, :], preferred_element_type=F32)
            total = d if total is None else total + d
        prow[...] = total if g == 0 else prow[...] + total

    ag_end(0)
    p_terms(0)
    ag_step(2, 3)
    ag_end(1)
    p_terms(1)
    ag_end(2)
    p_terms(2)

    @pl.when(core == 0)
    def _():
        pcol[0:BLK, :] = prow[...]
        pcol[1280:STK, :] = jnp.zeros((BLK, 256), F32)

    @pl.when(core == 1)
    def _():
        pcol[1280:STK, :] = prow[...]

    lanes = pl.ds(al(core * 128, 128), 128)
    psend[...] = pcol[:, pl.ds(al(128 - core * 128, 128), 128)].astype(BF)
    share = start("share", psend, precv, dev(fc=1))
    share.wait_recv()
    mcopies = []
    for i, at, where in ((0, BLK, dev(dx=1)), (1, 2 * BLK, dev(dx=2)), (2, 1280, dev(fy=1))):
        mout[i] = (pcol[at : at + BLK, lanes] + precv[at : at + BLK, :].astype(F32)).astype(BF)
        mcopies.append(start(f"m{i}", mout.at[i], mrecv.at[i], where))
    total = pcol[own, lanes] + precv[own, :].astype(F32)
    for i, c in enumerate(mcopies):
        c.wait_recv()
        total = total + mrecv[i].astype(F32)
    proj[...] = total.astype(BF).astype(F32)

    grad_copy.wait()
    acc = [jnp.zeros((16, 128), F32) for _ in range(3)]
    energy = jnp.zeros((1, 128), F32)

    def body(step, carry):
        a0, a1, a2, e = carry
        rows = pl.ds(al(step * 16, 16), 16)
        pr = proj[rows, :]
        at = ats[core, rows, :].astype(F32)
        e = e + jnp.sum(pr * at, axis=0, keepdims=True)
        out = []
        for c, a in enumerate((a0, a1, a2)):
            for r in range(16):
                a = a + grads[c, step * 16 + r].astype(F32) * pr[r : r + 1, :]
            out.append(a)
        return (*out, e)

    a0, a1, a2, energy = lax.fori_loop(0, 25, body, (*acc, energy))
    pr = proj[400:416, :]
    at = ats[core, 400:416, :].astype(F32)
    energy = energy + jnp.sum(pr * at, axis=0, keepdims=True)
    out = []
    for c, a in enumerate((a0, a1, a2)):
        for r in range(10):
            a = a + grads[c, 400 + r].astype(F32) * pr[r : r + 1, :]
        out.append(a)

    for c in range(3):
        pair_parts[8, c * 16 : (c + 1) * 16, :] = out[c]
    pair_parts[8, 48:49, :] = energy
    scopies = []
    for i, (dx, fy) in enumerate(((1, 0), (-1, 0), (2, 0), (0, 1), (1, 1), (-1, 1), (2, 1))):
        scopies.append(start(f"q{i}", pair_parts.at[8], pair_parts.at[col], dev(dx=dx, fy=fy)))
    pair_parts[col] = pair_parts[8]
    for c in scopies:
        c.wait_recv()
    summed = pair_parts[0]
    for i in range(1, 8):
        summed = summed + pair_parts[i]
    active = jnp.where(spec_ref[...] == 0, 1.0, 0.0)
    out_ref[3:4, :] = summed[48:49, :] * active
    for c in range(3):
        pairs[c] = summed[c * 16 : (c + 1) * 16, :] * active
    own = jnp.sum(pairs[...], axis=1)
    for n in range(16):
        mrow[0:3, n * 128 : (n + 1) * 128] = pairs[:, n, :]
    high = mrow[...].astype(BF)
    low = (mrow[...] - high.astype(F32)).astype(BF)
    dims = (((1,), (1,)), ((), ()))
    spread = lax.dot_general(high, onehot[...], dims, preferred_element_type=F32)
    spread = spread + lax.dot_general(low, onehot[...], dims, preferred_element_type=F32)
    fsend[0] = spread[:, 0:128]
    fsend[1] = spread[:, 256:384]
    fb = start("fb", fsend.at[0], frecv.at[0], before)
    fa = start("fa", fsend.at[1], frecv.at[1], after)
    center = 2.0 * own - 2.0 * spread[0:3, 128:256]
    fb.wait_recv()
    fa.wait_recv()
    out_ref[0:3, :] = center - 2.0 * frecv[0, 0:3, :] - 2.0 * frecv[1, 0:3, :]

    assert len(names) <= NSEM
    for c in sent:
        c.wait_send()


def shards(env_desc, alpha, atom_desc, desc_grad, species, neighbors):
    vm = pl.BlockSpec(memory_space=pltpu.VMEM)
    V = pltpu.VMEM
    out = pl.pallas_call(
        kernel,
        out_shape=jax.ShapeDtypeStruct((4, 128), F32),
        in_specs=[pl.BlockSpec(memory_space=pl.ANY), vm, vm, vm, vm, pl.BlockSpec(memory_space=pl.ANY)],
        out_specs=vm,
        scratch_shapes=[
            V((410, 2048), BF), V((896, 2048), BF), V((512, 1024), BF), V((BLK, 1024), BF), V((BLK, 2048), BF),
            V((2, BLK, 2048), BF), V((2, ROWS, 128), F32), V((ROWS, 128), BF), V((ROWS, 128), BF),
            V((4, 528, 128), BF), V((4, 528, 128), BF), V((3, 528, 128), BF), V((3, 528, 128), BF),
            V((528, 128), F32), V((528, 128), BF), V((528, 128), BF), V((ROWS, 128), BF),
            V((2, STK, 128), BF), V((1280, 256), BF), V((BLK, 256), BF),
            V((3, 410, 16, 128), BF), V((384, 2048), BF),
            V((BLK, 256), F32), V((STK, 256), F32), V((STK, 128), BF), V((STK, 128), BF),
            V((3, BLK, 128), BF), V((3, BLK, 128), BF), V((BLK, 128), F32),
            V((9, 56, 128), F32), V((3, 16, 128), F32), V((8, 2048), F32),
            V((2, 8, 128), F32), V((2, 8, 128), F32),
            pltpu.SemaphoreType.DMA((2,)), pltpu.SemaphoreType.DMA((NSEM,)), pltpu.SemaphoreType.DMA((NSEM,)),
        ],
        compiler_params=pltpu.CompilerParams(
            collective_id=0, has_side_effects=True, vmem_limit_bytes=58 * 2**20
        ),
    )(
        env_desc.T,
        alpha[None, :],
        atom_desc.T,
        species[None, :],
        neighbors.T,
        jnp.transpose(desc_grad, (2, 3, 1, 0)),
    )

    def outputs(both_ref, energy_ref, force_ref):
        energy_ref[...] = both_ref[3:4, :]
        force_ref[...] = both_ref[0:3, :]

    energies, forces = pl.pallas_call(
        outputs, out_shape=(jax.ShapeDtypeStruct((1, 128), F32), jax.ShapeDtypeStruct((3, 128), F32))
    )(out)
    return energies.reshape(128), forces


def solution(mesh):
    placed = (
        P("sp", "col"),
        P("sp"),
        P("sp", "col"),
        P("sp", None, None, "col"),
        P("sp"),
        P("sp", None),
    )
    return jax.shard_map(
        shards, mesh=mesh, in_specs=placed, out_specs=(P("sp"), P(None, "sp")), check_vma=False
    )
```

```python
import functools

import jax
import jax.numpy as jnp
from jax import lax
from jax.experimental import pallas as pl
from jax.experimental.pallas import tpu as pltpu
from jax.sharding import PartitionSpec as P

MESH = pl.DeviceIdType.MESH
BF = jnp.bfloat16
F32 = jnp.float32
BLK = 416
LO, HI = 256, 160
KC, KD = 512, 1024
ROW1 = BLK + LO
ROWA, ROWF, ROWH, ROWS = 4 * ROW1, 4 * ROW1 + 4 * HI, 4 * ROW1 + 4 * HI + 2 * BLK, 4608
CHS = (176, 160, 128, 112)
OFF = (0, 8 * 176, ROWA, ROWA + 8 * 128)
NLO, OLO, NHI, OHI, LANES = 416, 768, 1024, 1184, 1408
NSEM = 128
NT = (((1,), (1,)), ((), ()))
TN = (((0,), (0,)), ((), ()))


def kernel(
    env_ref, alpha_hbm, at_hbm, spec_hbm, nb_hbm, grad_ref,
    out_ref,
    alpha_ref, at_ref, spec_ref, nb_ref, env, r1, nhi, olo, ohi, relay_lo, relay_hi, part, uw, acc, osend, orecv, rsp, rrp, rsm, rrm, csum, ysend, yrecv, ball,
    ats, astack, arow, grads, onehot, prow, pcol, pown, psend, precv, mout, mrecv, proj, pairs, mrow, fsend, frecv,
    lsem, ssem, rsem, fsem,
):
    sp, col = lax.axis_index("sp"), lax.axis_index("col")
    core, yh, z = sp % 2, (sp // 2) % 2, sp // 4
    x, yl = col % 4, col // 4

    def dev(dx=0, fy=0, fh=0, dz=0, fc=0):
        a = 1 - yl if fy else yl
        h = 1 - yh if fh else yh
        k = 1 - core if fc else core
        return ((((z + dz + 8) % 8) * 2 + h) * 2 + k, a * 4 + (x + dx + 4) % 4)

    names = {}
    sent = []

    def copy(name, src, dst, where):
        i = names.setdefault(name, len(names))
        return pltpu.make_async_remote_copy(
            src_ref=src, dst_ref=dst, send_sem=ssem.at[i], recv_sem=rsem.at[i],
            device_id=where, device_id_type=MESH,
        )

    def start(name, src, dst, where):
        c = copy(name, src, dst, where)
        c.start()
        sent.append(c)
        return c

    def al(v, m):
        return pl.multiple_of(v, m)

    env_copy = pltpu.make_async_copy(env_ref, env, lsem.at[0])
    env_copy.start()
    small = []
    for i, (src, dst) in enumerate(((alpha_hbm, alpha_ref), (at_hbm, at_ref), (nb_hbm, nb_ref), (spec_hbm, spec_ref))):
        small.append(pltpu.make_async_copy(src, dst, lsem.at[2 + i]))
        small[-1].start()
    peers = [dev(dx=1), dev(dx=-1), dev(dx=2), dev(fy=1), dev(dx=1, fy=1), dev(dx=-1, fy=1), dev(dx=2, fy=1)]
    peers += [dev(fc=1), dev(fh=1), dev(dz=1), dev(dz=-1)]
    across = [(col + j) % 8 for j in range(8)]
    before, after = (sp + 31) % 32, (sp + 1) % 32
    peers += [(s, c) for s in (before, after) for c in across]
    barrier = pltpu.get_barrier_semaphore()
    for p in peers:
        pl.semaphore_signal(barrier, inc=1, device_id=p, device_id_type=MESH)
    env_copy.wait()
    grad_copy = pltpu.make_async_copy(grad_ref, grads, lsem.at[1])
    grad_copy.start()
    r1[400:416, :] = jnp.zeros((16, 2048), BF)
    r1[0:400, :] = env[0:400, :]
    r1[400:410, :] = env[400:410, :]
    pl.semaphore_wait(barrier, len(peers))

    def order(at_x):
        t = jnp.where(at_x % 4 >= 2, 0, 1024)
        return [al(o, KC) for o in (t, t + KC, 1024 - t, 1024 - t + KC)]

    ks = order(x)
    ks_left = order(x + 3)
    kh = [al(ks[0], KD), al(ks[2], KD)]
    kh_left = [al(ks_left[0], KD), al(ks_left[2], KD)]
    first = al(jnp.where(x < 2, 0, 1024), KD)
    own = slice(0, BLK)
    low_rows, high_rows = slice(0, LO), slice(LO, BLK)
    ys, yh_parts, os, rs = [], [], [], []
    for i in range(4):
        ys.append(start(f"y{i}", r1.at[low_rows, pl.ds(ks[i], KC)], part.at[low_rows, pl.ds(ks[i], KC)], dev(fy=1)))
        start(f"n{i}", r1.at[low_rows, pl.ds(ks_left[i], KC)], r1.at[NLO : NLO + LO, pl.ds(ks_left[i], KC)], dev(dx=-1))
        if i < 2:
            os.append(start(f"o{i}", r1.at[low_rows, pl.ds(al(first + i * KC, KC), KC)], relay_lo.at[:, pl.ds(i * KC, KC)], dev(dx=1)))
    for i in range(2):
        yh_parts.append(start(f"yh{i}", r1.at[high_rows, pl.ds(kh[i], KD)], part.at[high_rows, pl.ds(kh[i], KD)], dev(fy=1)))
        start(f"nh{i}", r1.at[high_rows, pl.ds(kh_left[i], KD)], nhi.at[0:HI, pl.ds(kh_left[i], KD)], dev(dx=-1))

    def n_wait(i):
        copy(f"n{i}", r1.at[low_rows, pl.ds(ks[i], KC)], r1.at[NLO : NLO + LO, pl.ds(ks[i], KC)], dev(dx=-1)).wait_recv()

    def nh_wait(i):
        copy(f"nh{i}", r1.at[high_rows, pl.ds(kh[i], KD)], nhi.at[0:HI, pl.ds(kh[i], KD)], dev(dx=-1)).wait_recv()

    def pass_on(i):
        os[i].wait_recv()
        if i < 2:
            rs.append(start(f"r{i}", relay_lo.at[:, pl.ds(i * KC, KC)], olo.at[:, pl.ds(i * KC, KC)], dev(dx=1)))
        else:
            lanes = pl.ds((i - 2) * KC, KC)
            rs.append(start(f"r{i}", relay_hi.at[:, lanes], ohi.at[32 : 32 + HI, lanes], dev(dx=1)))

    def o_high(i):
        lanes = pl.ds((i - 2) * KC, KC)
        src = r1.at[high_rows, pl.ds(al(first + (i - 2) * KC, KC), KC)]
        os.append(start(f"o{i}", src, relay_hi.at[:, lanes], dev(dx=1)))

    r1[NLO + LO : OLO, :] = jnp.zeros((OLO - NLO - LO, 2048), BF)
    nhi[HI:256, :] = jnp.zeros((256 - HI, 2048), BF)
    ohi[0:32, :] = jnp.zeros((32, 1024), BF)
    ohi[32 + HI : 256, :] = jnp.zeros((224 - HI, 1024), BF)
    for c in small:
        c.wait()
    uw[own, :] = (r1[own, :].astype(F32) * alpha_ref[...]).astype(BF)
    slots = lax.broadcasted_iota(jnp.int32, (384, 128), 0)
    for n in range(16):
        onehot[:, n * 128 : (n + 1) * 128] = jnp.where(slots == nb_ref[n : n + 1, :], 1.0, 0.0).astype(BF)
    mrow[...] = jnp.zeros_like(mrow)
    prow[...] = jnp.zeros_like(prow)
    pcol[...] = jnp.zeros_like(pcol)
    for c in (0, 1):
        acc[c, ROWH + BLK : ROWS, :] = jnp.zeros((ROWS - ROWH - BLK, 128), F32)
    ats[core, 400:416, :] = jnp.zeros((16, 128), BF)
    ats[core, 0:400, :] = at_ref[0:400, :]
    ats[core, 400:410, :] = at_ref[400:410, :]

    filled = set()

    def add(c, row, v):
        at = slice(row, row + v.shape[0])
        acc[c, at, :] = acc[c, at, :] + v if (c, row) in filled else v
        filled.add((c, row))

    def weigh(rows, k, n):
        at = slice(BLK + rows.start, BLK + rows.stop)
        uw[at, pl.ds(k, n)] = (part[rows, pl.ds(k, n)].astype(F32) * alpha_ref[:, pl.ds(k, n)]).astype(BF)

    def product(rows, rhs, r0, k, rk, n):
        return lax.dot_general(
            uw[rows, pl.ds(k, n)], rhs[r0 : r0 + 256, pl.ds(rk, n)], NT, preferred_element_type=F32
        )

    def panels(v, t, base, stride):
        for j in (0, 1):
            add((t + j) // 4, base + (t + j) % 4 * stride, v[:, j * 128 : (j + 1) * 128])

    front, back, every = slice(0, ROW1), slice(ROW1, 2 * BLK), slice(0, 2 * BLK)

    def low_step(i):
        ys[i].wait_recv()
        n_wait(i)
        weigh(low_rows, ks[i], KC)
        for t in (0, 2, 4):
            panels(product(front, r1, t * 128, ks[i], ks[i], KC), t, 0, ROW1)

    def low_opposite(j):
        rs[j].wait_recv()
        panels(product(front, olo, 0, ks[j], j * KC, KC), 6, 0, ROW1)

    def high_step(i):
        yh_parts[i].wait_recv()
        nh_wait(i)
        weigh(high_rows, kh[i], KD)
        for t in (0, 2, 4):
            panels(product(back, r1, t * 128, kh[i], kh[i], KD), t, ROWA, HI)
        if i == 0:
            panels(product(back, olo, 0, kh[0], 0, KD), 6, ROWA, HI)
        v = product(every, nhi, 0, kh[i], kh[i], KD)
        add(0, ROWF, v[:, 0:128])
        add(0, ROWH, v[0:BLK, 128:256])
        add(1, ROWH, v[BLK : 2 * BLK, 128:256])

    def high_opposite():
        rs[2].wait_recv()
        rs[3].wait_recv()
        v = product(every, ohi, 0, kh[0], 0, KD)
        add(0, ROWH, v[0:BLK, 0:128])
        add(1, ROWH, v[BLK : 2 * BLK, 0:128])
        add(1, ROWF, v[:, 128:256])

    cores = []

    def core_send(rows):
        osend[rows, :] = acc[1 - core, rows, :].astype(BF)
        cores.append(start(f"core{rows.start}", osend.at[rows, :], orecv.at[rows, :], dev(fc=1)))

    def chunk(g, d):
        return pl.ds(al(OFF[g] + ((d + 8) % 8) * CHS[g], 16), CHS[g])

    def slot(g):
        return slice(OFF[g] // 8, OFF[g] // 8 + CHS[g])

    def local(g, d):
        return acc[core, chunk(g, d), :] + orecv[chunk(g, d), :].astype(F32)

    live = {}

    def ring(g, far):
        return (1 if far == 4 else -1) * (1 if g % 2 == 0 else -1)

    def rs_send(g, s):
        if s == 0 and g % 2 == 0:
            cores[g // 2].wait_recv()
        for far, sbuf, rbuf in ((4, rsp, rrp), (3, rsm, rrm)):
            if s >= far:
                continue
            way = ring(g, far)
            v = local(g, z + way * (far - s))
            if s:
                live[g, far, s - 1].wait_recv()
                v = v + rbuf[s - 1, slot(g), :].astype(F32)
            sbuf[s, slot(g), :] = v.astype(BF)
            live[g, far, s] = start(f"s{far}{g}{s}", sbuf.at[s, slot(g), :], rbuf.at[s, slot(g), :], dev(dz=way))

    ycopies = {}

    def rs_end(g):
        live[g, 4, 3].wait_recv()
        live[g, 3, 2].wait_recv()
        v = local(g, z) + rrp[3, slot(g), :].astype(F32) + rrm[2, slot(g), :].astype(F32)
        csum[slot(g), :] = v
        ysend[slot(g), :] = v.astype(BF)
        ycopies[g] = start(f"h{g}", ysend.at[slot(g), :], yrecv.at[slot(g), :], dev(fh=1))

    def ag_start(g):
        ycopies[g].wait_recv()
        ball[chunk(g, z), :] = (csum[slot(g), :] + yrecv[slot(g), :].astype(F32)).astype(BF)
        ag_step(g, 0)

    def ag_copy(g, s, far, recv=0):
        ref = ball.at[chunk(g, z - ring(g, far) * (s + recv)), :]
        return copy(f"g{far}{g}{s}", ref, ref, dev(dz=ring(g, far)))

    def ag_step(g, s):
        for far in (4, 3):
            if s < far:
                if s:
                    ag_copy(g, s - 1, far, 1).wait_recv()
                c = ag_copy(g, s, far)
                c.start()
                sent.append(c)

    def ag_end(g):
        for far in (4, 3):
            ag_copy(g, far - 1, far, 1).wait_recv()

    pass_on(0)
    o_high(2)
    low_step(0)
    pass_on(1)
    o_high(3)
    low_step(1)
    low_step(2)
    low_opposite(0)
    low_step(3)
    low_opposite(1)
    core_send(slice(0, ROWA))
    pass_on(2)
    rs_send(0, 0)
    rs_send(1, 0)
    pass_on(3)
    rs_send(0, 1)
    rs_send(1, 1)
    high_step(0)
    rs_send(0, 2)
    rs_send(1, 2)
    high_step(1)
    high_opposite()
    core_send(slice(ROWA, ROWS))
    own_at = ats.at[core, own, :]
    acopies = [
        start("an", own_at, ats.at[core, BLK : 2 * BLK, :], dev(dx=-1)),
        start("ao", own_at, ats.at[core, 2 * BLK : 3 * BLK, :], dev(dx=2)),
        start("ap", own_at, ats.at[core, 3 * BLK : 4 * BLK, :], dev(fy=1)),
    ]
    rs_send(0, 3)
    rs_send(1, 3)
    rs_send(2, 0)
    rs_send(3, 0)
    rs_end(0)
    rs_end(1)
    rs_send(2, 1)
    rs_send(3, 1)
    ag_start(0)
    ag_start(1)
    rs_send(2, 2)
    rs_send(3, 2)
    ag_step(0, 1)
    ag_step(1, 1)
    for c in acopies:
        c.wait_recv()
    hand = start("hand", ats.at[core], ats.at[core], dev(fc=1))
    rs_send(2, 3)
    rs_send(3, 3)
    ag_step(0, 2)
    ag_step(1, 2)
    rs_end(2)
    rs_end(3)
    ag_step(0, 3)
    ag_step(1, 3)
    copy("hand", ats.at[1 - core], ats.at[1 - core], dev(fc=1)).wait_recv()

    def block(i, rows=own):
        return slice(i * BLK + rows.start, i * BLK + rows.stop)

    both = jnp.concatenate([ats[0], ats[1]], axis=1)
    arow[own, :] = both[block(0), :]
    arow[BLK : 2 * BLK, :] = both[block(3), :]
    astack[own, :] = both[block(0), :]
    astack[NLO : NLO + LO, :] = both[block(1, low_rows), :]
    astack[NLO + LO : OLO, :] = jnp.zeros((OLO - NLO - LO, 256), BF)
    astack[OLO:NHI, :] = both[block(2, low_rows), :]
    astack[NHI:OHI, :] = both[block(1, high_rows), :]
    astack[OHI : OHI + HI, :] = both[block(2, high_rows), :]
    astack[OHI + HI : LANES, :] = jnp.zeros((LANES - OHI - HI, 256), BF)
    ag_start(2)
    ag_start(3)

    def dot(a, b):
        return jnp.dot(a, b, preferred_element_type=F32)

    def turned(a, b):
        return lax.dot_general(a, b, TN, preferred_element_type=F32)

    def p_first():
        ag_end(0)
        ag_end(1)

        @pl.when(core == 0)
        def _():
            total = jnp.zeros((BLK, 256), F32)
            for q in range(4):
                own_part = ball[q * ROW1 : q * ROW1 + BLK, :]
                partner = ball[q * ROW1 + BLK : (q + 1) * ROW1, :]
                at = slice(q * 128, (q + 1) * 128)
                total = total + dot(own_part, astack[at, :])
                terms = turned(partner, arow[BLK:ROW1, :])
                if q == 3:
                    next_only = lax.broadcasted_iota(jnp.int32, (128, 256), 0) >= BLK - 384
                    terms = terms + jnp.where(next_only, turned(own_part, arow[own, :]), 0.0)
                    prow[BLK:ROW1, :] = dot(partner, jnp.where(next_only, astack[at, :].astype(F32), 0.0).astype(BF))
                pcol[at, :] = terms
            prow[own, :] = total

        @pl.when(core == 1)
        def _():
            total = jnp.zeros((ROW1, 256), F32)
            for q in range(4):
                beta = ball[q * ROW1 : (q + 1) * ROW1, :]
                at = slice((4 + q) * 128, (5 + q) * 128)
                total = total + dot(beta, astack[at, :])
                pcol[at, :] = turned(beta, arow[front, :])
            prow[front, :] = total

    def p_second():
        ag_end(2)
        ag_end(3)
        full = ball[ROWF:ROWH, :]
        half = ball[ROWH : ROWH + BLK, :]
        mid = slice(NHI + 128, NHI + 256)

        def ends(at, rows):
            prow[...] = prow[...] + dot(full, astack[at, :])
            prow[rows, :] = prow[rows, :] + dot(half, astack[mid, :])
            pcol[at, :] = turned(full, arow[...])
            pcol[mid, :] = turned(half, arow[rows, :])

        def rest(c):
            for q in range(4):
                beta = ball[ROWA + q * HI : ROWA + (q + 1) * HI, :]
                at = slice((4 * c + q) * 128, (4 * c + q + 1) * 128)
                pcol[at, :] = pcol[at, :] + turned(beta, arow[back, :])
                if c == 1:
                    prow[back, :] = prow[back, :] + dot(beta, astack[at, :])
                elif q == 3:
                    next_only = lax.broadcasted_iota(jnp.int32, (128, 256), 0) >= BLK - 384
                    a = jnp.where(next_only, astack[at, :].astype(F32), 0.0).astype(BF)
                    prow[back, :] = prow[back, :] + dot(beta, a)

        @pl.when(core == 0)
        def _():
            ends(slice(NHI, NHI + 128), own)
            rest(0)

        @pl.when(core == 1)
        def _():
            ends(slice(NHI + 256, LANES), slice(BLK, 2 * BLK))
            rest(1)

    ag_step(2, 1)
    ag_step(3, 1)
    ag_step(2, 2)
    ag_step(3, 2)
    p_first()
    ag_step(2, 3)
    ag_step(3, 3)
    p_second()

    pieces = (
        (0, prow, 0, BLK), (0, pcol, 0, BLK), (BLK, pcol, NLO, LO), (BLK + LO, pcol, NHI, HI),
        (2 * BLK, pcol, OLO, LO), (2 * BLK + LO, pcol, OHI, HI), (3 * BLK, prow, BLK, BLK),
    )
    mine = pl.ds(al(core * 128, 128), 128)
    other = pl.ds(al(128 - core * 128, 128), 128)
    for lanes, keep in ((other, False), (mine, True)):
        for to, src, at, n in pieces:
            v = src[at : at + n, lanes]
            if to == 0 and src is pcol:
                v = v + prow[own, lanes]
            elif to == 0:
                continue
            if keep:
                pown[to : to + n, :] = v
            else:
                psend[to : to + n, :] = v.astype(BF)
        if not keep:
            share = start("share", psend, precv, dev(fc=1))
    share.wait_recv()
    mcopies = []
    for i, where in ((1, dev(dx=2)), (0, dev(dx=1)), (2, dev(fy=1))):
        at = slice((i + 1) * BLK, (i + 2) * BLK)
        mout[i] = (pown[at, :] + precv[at, :].astype(F32)).astype(BF)
        mcopies.append((i, start(f"m{i}", mout.at[i], mrecv.at[i], where)))
    total = pown[own, :] + precv[own, :].astype(F32)
    for i, c in mcopies:
        c.wait_recv()
        total = total + mrecv[i].astype(F32)
    proj[...] = total.astype(BF).astype(F32)

    grad_copy.wait()
    zeros = [jnp.zeros((16, 128), F32) for _ in range(3)]
    energy = jnp.zeros((1, 128), F32)

    def body(step, carry):
        a0, a1, a2, e = carry
        rows = pl.ds(al(step * 16, 16), 16)
        pr = proj[rows, :]
        at = ats[core, rows, :].astype(F32)
        e = e + jnp.sum(pr * at, axis=0, keepdims=True)
        out = []
        for c, a in enumerate((a0, a1, a2)):
            for r in range(16):
                a = a + grads[c, step * 16 + r].astype(F32) * pr[r : r + 1, :]
            out.append(a)
        return (*out, e)

    a0, a1, a2, energy = lax.fori_loop(0, 25, body, (*zeros, energy))
    pr = proj[400:416, :]
    at = ats[core, 400:416, :].astype(F32)
    energy = energy + jnp.sum(pr * at, axis=0, keepdims=True)
    out = []
    for c, a in enumerate((a0, a1, a2)):
        for r in range(10):
            a = a + grads[c, 400 + r].astype(F32) * pr[r : r + 1, :]
        out.append(a)

    active = jnp.where(spec_ref[...] == 0, 1.0, 0.0)
    for c in range(3):
        pairs[c] = out[c] * active
    for n in range(16):
        mrow[0:3, n * 128 : (n + 1) * 128] = pairs[:, n, :]
    high = mrow[...].astype(BF)
    low = (mrow[...] - high.astype(F32)).astype(BF)
    spread = lax.dot_general(jnp.concatenate([high, low], axis=0), onehot[...], NT, preferred_element_type=F32)
    spread = -2.0 * (spread[0:8, :] + spread[8:16, :])
    fsend[0] = spread[:, 128:256]
    fsend[0, 0:3, :] = spread[0:3, 128:256] + 2.0 * jnp.sum(pairs[...], axis=1)
    fsend[0, 3:4, :] = energy * active
    fsend[1] = spread[:, 0:128]
    fsend[2] = spread[:, 256:384]

    for j in range(8):
        for kind, where in ((1, before), (2, after), (0, sp)):
            if j or kind:
                pltpu.make_async_remote_copy(
                    src_ref=fsend.at[kind], dst_ref=frecv.at[kind, col],
                    send_sem=fsem.at[min(kind, 1)], recv_sem=fsem.at[2 + min(kind, 1)],
                    device_id=(where, across[j]), device_id_type=MESH,
                ).start()
    frecv[0, col] = fsend[0]
    for c in sent:
        c.wait_send()
    fcopies = []
    for i, ref in ((0, frecv.at[0, 0:7]), (1, frecv.at[1:3])):
        fcopies.append(pltpu.make_async_remote_copy(
            src_ref=ref, dst_ref=ref, send_sem=fsem.at[i], recv_sem=fsem.at[2 + i], device_id=(sp, across[1]), device_id_type=MESH,
        ))
    for c in fcopies:
        c.wait_recv()
    summed = jnp.zeros((8, 128), F32)
    for kind in range(3):
        for j in range(8):
            summed = summed + frecv[kind, j]
    out_ref[...] = summed[0:4, :]

    assert len(names) <= NSEM
    for c in fcopies:
        c.wait_send()


def shards(env_desc, alpha, atom_desc, desc_grad, species, neighbors):
    vm = pl.BlockSpec(memory_space=pltpu.VMEM)
    V = pltpu.VMEM
    out = pl.pallas_call(
        kernel,
        out_shape=jax.ShapeDtypeStruct((4, 128), F32),
        in_specs=[pl.BlockSpec(memory_space=pl.ANY)] * 6,
        out_specs=vm,
        scratch_shapes=[
            V((1, 2048), F32), V((410, 128), BF), V((1, 128), jnp.int32), V((16, 128), jnp.int32),
            V((410, 2048), BF), V((OLO, 2048), BF), V((256, 2048), BF), V((LO, 1024), BF), V((256, 1024), BF),
            V((LO, 1024), BF), V((HI, 1024), BF), V((BLK, 2048), BF),
            V((2 * BLK, 2048), BF), V((2, ROWS, 128), F32), V((ROWS, 128), BF), V((ROWS, 128), BF),
            V((4, 576, 128), BF), V((4, 576, 128), BF), V((3, 576, 128), BF), V((3, 576, 128), BF),
            V((576, 128), F32), V((576, 128), BF), V((576, 128), BF), V((ROWS, 128), BF),
            V((2, 4 * BLK, 128), BF), V((LANES, 256), BF), V((2 * BLK, 256), BF),
            V((3, 410, 16, 128), BF), V((384, 2048), BF),
            V((2 * BLK, 256), F32), V((LANES, 256), F32), V((4 * BLK, 128), F32), V((4 * BLK, 128), BF), V((4 * BLK, 128), BF),
            V((3, BLK, 128), BF), V((3, BLK, 128), BF), V((BLK, 128), F32),
            V((3, 16, 128), F32), V((8, 2048), F32),
            V((3, 8, 128), F32), V((3, 8, 8, 128), F32),
            pltpu.SemaphoreType.DMA((6,)), pltpu.SemaphoreType.DMA((NSEM,)), pltpu.SemaphoreType.DMA((NSEM,)), pltpu.SemaphoreType.DMA((4,)),
        ],
        compiler_params=pltpu.CompilerParams(
            collective_id=0, has_side_effects=True, vmem_limit_bytes=58 * 2**20
        ),
    )(
        env_desc.T,
        alpha[None, :],
        atom_desc.T,
        species[None, :],
        neighbors.T,
        jnp.transpose(desc_grad, (2, 3, 1, 0)),
    )

    def outputs(both_ref, energy_ref, force_ref):
        energy_ref[...] = both_ref[3:4, :]
        force_ref[...] = both_ref[0:3, :]

    energies, forces = pl.pallas_call(
        outputs, out_shape=(jax.ShapeDtypeStruct((1, 128), F32), jax.ShapeDtypeStruct((3, 128), F32))
    )(out)
    return energies.reshape(128), forces


def solution(mesh):
    placed = (
        P("sp", "col"),
        P("sp"),
        P("sp", "col"),
        P("sp", None, None, "col"),
        P("sp"),
        P("sp", None),
    )
    return jax.shard_map(
        shards, mesh=mesh, in_specs=placed, out_specs=(P("sp"), P(None, "sp")), check_vma=False
    )
```

```python
import functools

import jax
import jax.numpy as jnp
from jax import lax
from jax.experimental import pallas as pl
from jax.experimental.pallas import tpu as pltpu
from jax.sharding import PartitionSpec as P

MESH = pl.DeviceIdType.MESH
BF = jnp.bfloat16
F32 = jnp.float32
BLK = 416
LO, HI = 288, 128
KC = 512
ROW1 = BLK + LO
ROWA, ROWS = 4 * ROW1, 4224
ROWF = ROWA + 4 * HI
ROWZ = ROWF + 2 * BLK
CHS = (176, 176, 96, 80)
OFF = (0, 1408, ROWA, ROWA + 8 * 96)
NLO, OLO, OEND, NHI, OHI, LANES = 416, 704, 992, 1024, 1152, 1280
NSEM = 128
NT = (((1,), (1,)), ((), ()))
TN = (((0,), (0,)), ((), ()))


def kernel(
    env_ref, alpha_hbm, at_hbm, spec_hbm, nb_hbm, grad_ref,
    out_ref,
    alpha_ref, at_ref, spec_ref, nb_ref, env, r1, nhi, olo, ohi, relay_lo, relay_hi, part, uw, acc, osend, orecv, rsend, rrecv, csum, ysend, yrecv, ball,
    ats, astack, arow, grads, onehot, prow, pcol, pown, psend, precv, mout, mrecv, proj, pairs, mrow, fsend, frecv,
    lsem, ssem, rsem, fsem,
):
    sp, col = lax.axis_index("sp"), lax.axis_index("col")
    core, yh, z = sp % 2, (sp // 2) % 2, sp // 4
    x, yl = col % 4, col // 4

    def dev(dx=0, fy=0, fh=0, dz=0, fc=0):
        a = 1 - yl if fy else yl
        h = 1 - yh if fh else yh
        k = 1 - core if fc else core
        return ((((z + dz + 8) % 8) * 2 + h) * 2 + k, a * 4 + (x + dx + 4) % 4)

    names = {}
    sent = []

    def copy(name, src, dst, where):
        i = names.setdefault(name, len(names))
        return pltpu.make_async_remote_copy(
            src_ref=src, dst_ref=dst, send_sem=ssem.at[i], recv_sem=rsem.at[i],
            device_id=where, device_id_type=MESH,
        )

    def start(name, src, dst, where):
        c = copy(name, src, dst, where)
        c.start()
        sent.append(c)
        return c

    def al(v, m):
        return pl.multiple_of(v, m)

    env_copy = pltpu.make_async_copy(env_ref, env, lsem.at[0])
    env_copy.start()
    small = []
    for i, (src, dst) in enumerate(((alpha_hbm, alpha_ref), (at_hbm, at_ref), (nb_hbm, nb_ref), (spec_hbm, spec_ref))):
        small.append(pltpu.make_async_copy(src, dst, lsem.at[2 + i]))
        small[-1].start()
    peers = [dev(dx=1), dev(dx=-1), dev(dx=2), dev(fy=1), dev(dx=1, fy=1), dev(dx=-1, fy=1), dev(dx=2, fy=1)]
    peers += [dev(fc=1), dev(fh=1), dev(dz=1), dev(dz=-1), dev(dz=2), dev(dz=-2)]
    across = [(col + j) % 8 for j in range(8)]
    before, after = (sp + 31) % 32, (sp + 1) % 32
    peers += [(s, c) for s in (before, after) for c in across]
    barrier = pltpu.get_barrier_semaphore()
    for p in peers:
        pl.semaphore_signal(barrier, inc=1, device_id=p, device_id_type=MESH)
    env_copy.wait()
    grad_copy = pltpu.make_async_copy(grad_ref, grads, lsem.at[1])
    grad_copy.start()
    for k in range(4):
        lanes = slice(k * KC, (k + 1) * KC)
        r1[k, 400:416, :] = jnp.zeros((16, KC), BF)
        r1[k, 0:400, :] = env[0:400, lanes]
        r1[k, 400:410, :] = env[400:410, lanes]
    pl.semaphore_wait(barrier, len(peers))

    def order(at_x):
        t = jnp.where(at_x % 4 >= 2, 0, 2)
        return [t, t + 1, 2 - t, 3 - t]

    ks = order(x)
    ks_left = order(x + 3)
    first = jnp.where(x < 2, 0, 2)
    own = slice(0, BLK)
    low_rows, high_rows = slice(0, LO), slice(LO, BLK)
    ys, yh_parts, os, rs = [], [], [], []
    for i in range(4):
        ys.append(start(f"y{i}", r1.at[ks[i], low_rows, :], part.at[ks[i], low_rows, :], dev(fy=1)))
        start(f"n{i}", r1.at[ks_left[i], low_rows, :], r1.at[ks_left[i], NLO : NLO + LO, :], dev(dx=-1))
        if i < 2:
            os.append(start(f"o{i}", r1.at[first + i, low_rows, :], relay_lo.at[i], dev(dx=1)))
    for i in range(4):
        yh_parts.append(start(f"yh{i}", r1.at[ks[i], high_rows, :], part.at[ks[i], high_rows, :], dev(fy=1)))
        start(f"nh{i}", r1.at[ks_left[i], high_rows, :], nhi.at[ks_left[i]], dev(dx=-1))

    def n_wait(i):
        copy(f"n{i}", r1.at[ks[i], low_rows, :], r1.at[ks[i], NLO : NLO + LO, :], dev(dx=-1)).wait_recv()

    def nh_wait(i):
        copy(f"nh{i}", r1.at[ks[i], high_rows, :], nhi.at[ks[i]], dev(dx=-1)).wait_recv()

    def pass_on(i):
        os[i].wait_recv()
        if i < 2:
            rs.append(start(f"r{i}", relay_lo.at[i], olo.at[i, 64 : 64 + LO, :], dev(dx=1)))
        else:
            rs.append(start(f"r{i}", relay_hi.at[i - 2], ohi.at[i - 2], dev(dx=1)))

    def o_high(i):
        os.append(start(f"o{i}", r1.at[first + i - 2, high_rows, :], relay_hi.at[i - 2], dev(dx=1)))

    for k in range(4):
        r1[k, OLO:768, :] = jnp.zeros((768 - OLO, KC), BF)
    for k in range(2):
        olo[k, 0:64, :] = jnp.zeros((64, KC), BF)
        olo[k, 64 + LO : 384, :] = jnp.zeros((320 - LO, KC), BF)
    for c in small:
        c.wait()
    for k in range(4):
        uw[k, own, :] = (r1[k, own, :].astype(F32) * alpha_ref[:, k * KC : (k + 1) * KC]).astype(BF)
    slots = lax.broadcasted_iota(jnp.int32, (384, 128), 0)
    for n in range(16):
        onehot[:, n * 128 : (n + 1) * 128] = jnp.where(slots == nb_ref[n : n + 1, :], 1.0, 0.0).astype(BF)
    mrow[...] = jnp.zeros_like(mrow)
    prow[...] = jnp.zeros_like(prow)
    pcol[...] = jnp.zeros_like(pcol)
    for c in (0, 1):
        acc[c, ROWZ:ROWS, :] = jnp.zeros((ROWS - ROWZ, 128), F32)
    ats[core, 400:416, :] = jnp.zeros((16, 128), BF)
    ats[core, 0:400, :] = at_ref[0:400, :]
    ats[core, 400:410, :] = at_ref[400:410, :]

    filled = set()

    def add(c, row, v):
        at = slice(row, row + v.shape[0])
        acc[c, at, :] = acc[c, at, :] + v if (c, row) in filled else v
        filled.add((c, row))

    def weigh(rows, k):
        at = slice(BLK + rows.start, BLK + rows.stop)
        weight = alpha_ref[:, pl.ds(al(k * KC, KC), KC)]
        uw[k, at, :] = (part[k, rows, :].astype(F32) * weight).astype(BF)

    def product(rows, rhs, r0, n, steps):
        v = None
        for k, rk in steps:
            d = lax.dot_general(uw[k, rows, :], rhs[rk, r0 : r0 + n, :], NT, preferred_element_type=F32)
            v = d if v is None else v + d
        return v

    def panels(v, t, base, stride):
        for j in range(v.shape[1] // 128):
            add((t + j) // 4, base + (t + j) % 4 * stride, v[:, j * 128 : (j + 1) * 128])

    front, back, every = slice(0, ROW1), slice(ROW1, 2 * BLK), slice(0, 2 * BLK)

    def low_step(i):
        ys[i].wait_recv()
        n_wait(i)
        weigh(low_rows, ks[i])
        for t in (0, 2, 4):
            panels(product(front, r1, t * 128, 256, ((ks[i], ks[i]),)), t, 0, ROW1)

    def low_opposite(j):
        rs[j].wait_recv()
        panels(product(front, olo, 0, 384, ((ks[j], j),)), 5, 0, ROW1)

    def high_step(i):
        two = ks[2 * i : 2 * i + 2]
        for j, k in enumerate(two):
            yh_parts[2 * i + j].wait_recv()
            nh_wait(2 * i + j)
            weigh(high_rows, k)
        steps = [(k, k) for k in two]
        for t in (0, 2, 4):
            panels(product(back, r1, t * 128, 256, steps), t, ROWA, HI)
        if i == 0:
            panels(product(back, olo, 0, 384, ((ks[0], 0), (ks[1], 1))), 5, ROWA, HI)
        add(0, ROWF, product(every, nhi, 0, HI, steps))

    def high_opposite():
        rs[2].wait_recv()
        rs[3].wait_recv()
        add(1, ROWF, product(every, ohi, 0, HI, ((ks[0], 0), (ks[1], 1))))

    cores = []

    def core_send(rows):
        osend[rows, :] = acc[1 - core, rows, :].astype(BF)
        cores.append(start(f"core{rows.start}", osend.at[rows, :], orecv.at[rows, :], dev(fc=1)))

    def chunk(g, d):
        return pl.ds(al(OFF[g] + ((d + 8) % 8) * CHS[g], 16), CHS[g])

    def slot(g):
        return slice(OFF[g] // 8, OFF[g] // 8 + CHS[g])

    def local(g, d):
        return acc[core, chunk(g, d), :] + orecv[chunk(g, d), :].astype(F32)

    def side(g):
        return 1 if g % 2 == 0 else -1

    routes = ((-4, -2), (-3, -1), (3, 1), (-1, -1), (1, 1), (-2, -2), (2, 2))

    def rs_copy(g, i):
        return copy(f"s{g}{i}", rsend.at[i, slot(g), :], rrecv.at[i, slot(g), :], dev(dz=side(g) * routes[i][1]))

    def rs_first(g):
        if g % 2 == 0:
            cores[g // 2].wait_recv()
        for i in range(5):
            rsend[i, slot(g), :] = local(g, z + side(g) * routes[i][0]).astype(BF)
            c = rs_copy(g, i)
            c.start()
            sent.append(c)

    def rs_next(g):
        for i, came in ((5, (0, 1)), (6, (2,))):
            v = local(g, z + side(g) * routes[i][0])
            for j in came:
                rs_copy(g, j).wait_recv()
                v = v + rrecv[j, slot(g), :].astype(F32)
            rsend[i, slot(g), :] = v.astype(BF)
            c = rs_copy(g, i)
            c.start()
            sent.append(c)

    def first_rows(g, d):
        return pl.ds(al(g * OFF[1] + ((d + 8) % 8) * CHS[0], 16), CHS[0])

    def first_end():
        for g in (0, 1):
            for j in (3, 4, 5, 6):
                rs_copy(g, j).wait_recv()
        for g, keep in ((1 - yh, False), (yh, True)):
            rows, at = first_rows(g, z), pl.ds(al(g * CHS[0], 16), CHS[0])
            v = acc[core, rows, :] + orecv[rows, :].astype(F32)
            for j in (3, 4, 5, 6):
                v = v + rrecv[j, at, :].astype(F32)
            if keep:
                csum[0 : CHS[0], :] = v
            else:
                ysend[0 : CHS[0], :] = v.astype(BF)
                ycopies[0] = start("h0", ysend.at[0 : CHS[0], :], yrecv.at[0 : CHS[0], :], dev(fh=1))

    ycopies = {}

    def rs_end(g):
        v = local(g, z)
        for j in (3, 4, 5, 6):
            rs_copy(g, j).wait_recv()
            v = v + rrecv[j, slot(g), :].astype(F32)
        csum[slot(g), :] = v
        ysend[slot(g), :] = v.astype(BF)
        ycopies[g] = start(f"h{g}", ysend.at[slot(g), :], yrecv.at[slot(g), :], dev(fh=1))

    legs = ((0, 2), (0, -2), (0, 1), (0, -1), (-2, 2), (-2, 1), (2, -1))

    turn = 1 - 2 * core

    def ag_copy(g, i, recv=0):
        at, to = legs[i]
        if g == 0:
            ref = ball.at[first_rows(yh, z + turn * (at - recv * to)), :]
            return copy(f"g{g}{i}", ref, ref, dev(dz=turn * to))
        ref = ball.at[chunk(g, z + side(g) * (at - recv * to)), :]
        return copy(f"g{g}{i}", ref, ref, dev(dz=side(g) * to))

    def ag_send(g, legs_of):
        for i in legs_of:
            c = ag_copy(g, i)
            c.start()
            sent.append(c)

    def ag_first(g):
        ycopies[g].wait_recv()
        own_chunk = first_rows(yh, z) if g == 0 else chunk(g, z)
        ball[own_chunk, :] = (csum[slot(g), :] + yrecv[slot(g), :].astype(F32)).astype(BF)
        ag_send(g, (0, 1, 2, 3))
        if g == 0:
            over_send((7,))

    def ag_next(g):
        ag_copy(g, 0, 1).wait_recv()
        ag_send(g, (4, 5))
        ag_copy(g, 1, 1).wait_recv()
        ag_send(g, (6,))

    places = [at - to for at, to in legs] + [0]

    def over(i, where):
        ref = ball.at[first_rows(where, z + turn * places[i]), :]
        return copy(f"v{i}", ref, ref, dev(fh=1))

    def over_send(own_legs, waits=True):
        for i in own_legs:
            if i < 7 and waits:
                ag_copy(0, i, 1).wait_recv()
            c = over(i, yh)
            c.start()
            sent.append(c)

    def over_wait():
        for i in range(8):
            over(i, 1 - yh).wait_recv()

    def ag_end(g):
        for i in (2, 3, 4, 5, 6):
            ag_copy(g, i, 1).wait_recv()

    pass_on(0)
    low_step(0)
    pass_on(1)
    o_high(2)
    o_high(3)
    low_step(1)
    low_step(2)
    low_opposite(0)
    low_step(3)
    low_opposite(1)
    core_send(slice(0, ROWA))
    pass_on(2)
    rs_first(0)
    rs_first(1)
    pass_on(3)
    high_step(0)
    rs_next(0)
    rs_next(1)
    high_step(1)
    high_opposite()
    core_send(slice(ROWA, ROWS))
    rs_first(2)
    rs_first(3)
    first_end()
    own_at = ats.at[core, own, :]
    acopies = [
        start("an", own_at, ats.at[core, BLK : 2 * BLK, :], dev(dx=-1)),
        start("ao", own_at, ats.at[core, 2 * BLK : 3 * BLK, :], dev(dx=2)),
        start("ap", own_at, ats.at[core, 3 * BLK : 4 * BLK, :], dev(fy=1)),
    ]
    rs_next(2)
    rs_next(3)
    ag_first(0)
    for c in acopies:
        c.wait_recv()
    hand = start("hand", ats.at[core], ats.at[core], dev(fc=1))
    rs_end(2)
    rs_end(3)
    ag_next(0)
    over_send((0, 1), False)
    over_send((2, 3))
    copy("hand", ats.at[1 - core], ats.at[1 - core], dev(fc=1)).wait_recv()

    def block(i, rows=own):
        return slice(i * BLK + rows.start, i * BLK + rows.stop)

    both = jnp.concatenate([ats[0], ats[1]], axis=1)
    arow[own, :] = both[block(0), :]
    arow[BLK : 2 * BLK, :] = both[block(3), :]
    astack[own, :] = both[block(0), :]
    astack[NLO:OLO, :] = both[block(1, low_rows), :]
    astack[OLO:OEND, :] = both[block(2, low_rows), :]
    astack[OEND:NHI, :] = jnp.zeros((NHI - OEND, 256), BF)
    astack[NHI:OHI, :] = both[block(1, high_rows), :]
    astack[OHI:LANES, :] = both[block(2, high_rows), :]
    ag_first(2)
    ag_first(3)
    over_send((4, 6, 5))

    def dot(a, b):
        return jnp.dot(a, b, preferred_element_type=F32)

    def turned(a, b):
        return lax.dot_general(a, b, TN, preferred_element_type=F32)

    def p_first():
        over_wait()

        @pl.when(core == 0)
        def _():
            total = jnp.zeros((BLK, 256), F32)
            for q in range(4):
                own_part = ball[q * ROW1 : q * ROW1 + BLK, :]
                partner = ball[q * ROW1 + BLK : (q + 1) * ROW1, :]
                at = slice(q * 128, (q + 1) * 128)
                total = total + dot(own_part, astack[at, :])
                terms = turned(partner, arow[BLK:ROW1, :])
                if q == 3:
                    next_only = lax.broadcasted_iota(jnp.int32, (128, 256), 0) >= BLK - 384
                    terms = terms + jnp.where(next_only, turned(own_part, arow[own, :]), 0.0)
                    prow[BLK:ROW1, :] = dot(partner, jnp.where(next_only, astack[at, :].astype(F32), 0.0).astype(BF))
                pcol[at, :] = terms
            prow[own, :] = total

        @pl.when(core == 1)
        def _():
            total = jnp.zeros((ROW1, 256), F32)
            for q in range(4):
                beta = ball[q * ROW1 : (q + 1) * ROW1, :]
                at = slice((4 + q) * 128, (5 + q) * 128)
                total = total + dot(beta, astack[at, :])
                pcol[at, :] = turned(beta, arow[front, :])
            prow[front, :] = total

    def p_second():
        ag_end(2)
        ag_end(3)
        full = ball[ROWF:ROWZ, :]

        def ends(at):
            prow[...] = prow[...] + dot(full, astack[at, :])
            pcol[at, :] = turned(full, arow[...])

        def rest(c):
            for q in range(4):
                beta = ball[ROWA + q * HI : ROWA + (q + 1) * HI, :]
                at = slice((4 * c + q) * 128, (4 * c + q + 1) * 128)
                pcol[at, :] = pcol[at, :] + turned(beta, arow[back, :])
                if c == 1:
                    prow[back, :] = prow[back, :] + dot(beta, astack[at, :])
                elif q == 3:
                    next_only = lax.broadcasted_iota(jnp.int32, (128, 256), 0) >= BLK - 384
                    a = jnp.where(next_only, astack[at, :].astype(F32), 0.0).astype(BF)
                    prow[back, :] = prow[back, :] + dot(beta, a)

        @pl.when(core == 0)
        def _():
            ends(slice(NHI, OHI))
            rest(0)

        @pl.when(core == 1)
        def _():
            ends(slice(OHI, LANES))
            rest(1)

    ag_next(2)
    ag_next(3)
    p_first()
    p_second()

    pieces = (
        (0, prow, 0, BLK), (0, pcol, 0, BLK), (BLK, pcol, NLO, LO), (BLK + LO, pcol, NHI, HI),
        (2 * BLK, pcol, OLO, LO), (2 * BLK + LO, pcol, OHI, HI), (3 * BLK, prow, BLK, BLK),
    )
    mine = pl.ds(al(core * 128, 128), 128)
    other = pl.ds(al(128 - core * 128, 128), 128)
    for lanes, keep in ((other, False), (mine, True)):
        for to, src, at, n in pieces:
            v = src[at : at + n, lanes]
            if to == 0 and src is pcol:
                v = v + prow[own, lanes]
            elif to == 0:
                continue
            if keep:
                pown[to : to + n, :] = v
            else:
                psend[to : to + n, :] = v.astype(BF)
        if not keep:
            share = start("share", psend, precv, dev(fc=1))
    share.wait_recv()
    mcopies = []
    for i, where in ((1, dev(dx=2)), (0, dev(dx=1)), (2, dev(fy=1))):
        at = slice((i + 1) * BLK, (i + 2) * BLK)
        mout[i] = (pown[at, :] + precv[at, :].astype(F32)).astype(BF)
        mcopies.append((i, start(f"m{i}", mout.at[i], mrecv.at[i], where)))
    total = pown[own, :] + precv[own, :].astype(F32)
    for i, c in mcopies:
        c.wait_recv()
        total = total + mrecv[i].astype(F32)
    proj[...] = total.astype(BF).astype(F32)

    grad_copy.wait()
    zeros = [jnp.zeros((16, 128), F32) for _ in range(3)]
    energy = jnp.zeros((1, 128), F32)

    def body(step, carry):
        a0, a1, a2, e = carry
        rows = pl.ds(al(step * 16, 16), 16)
        pr = proj[rows, :]
        at = ats[core, rows, :].astype(F32)
        e = e + jnp.sum(pr * at, axis=0, keepdims=True)
        out = []
        for c, a in enumerate((a0, a1, a2)):
            for r in range(16):
                a = a + grads[c, step * 16 + r].astype(F32) * pr[r : r + 1, :]
            out.append(a)
        return (*out, e)

    a0, a1, a2, energy = lax.fori_loop(0, 25, body, (*zeros, energy))
    pr = proj[400:416, :]
    at = ats[core, 400:416, :].astype(F32)
    energy = energy + jnp.sum(pr * at, axis=0, keepdims=True)
    out = []
    for c, a in enumerate((a0, a1, a2)):
        for r in range(10):
            a = a + grads[c, 400 + r].astype(F32) * pr[r : r + 1, :]
        out.append(a)

    active = jnp.where(spec_ref[...] == 0, 1.0, 0.0)
    for c in range(3):
        pairs[c] = out[c] * active
    for n in range(16):
        mrow[0:3, n * 128 : (n + 1) * 128] = pairs[:, n, :]
    high = mrow[...].astype(BF)
    low = (mrow[...] - high.astype(F32)).astype(BF)
    spread = lax.dot_general(jnp.concatenate([high, low], axis=0), onehot[...], NT, preferred_element_type=F32)
    spread = -2.0 * (spread[0:8, :] + spread[8:16, :])
    fsend[0] = spread[:, 128:256]
    fsend[0, 0:3, :] = spread[0:3, 128:256] + 2.0 * jnp.sum(pairs[...], axis=1)
    fsend[0, 3:4, :] = energy * active
    fsend[1] = spread[:, 0:128]
    fsend[2] = spread[:, 256:384]

    for j in range(8):
        for kind, where in ((1, before), (2, after), (0, sp)):
            if j or kind:
                pltpu.make_async_remote_copy(
                    src_ref=fsend.at[kind], dst_ref=frecv.at[kind, col],
                    send_sem=fsem.at[min(kind, 1)], recv_sem=fsem.at[2 + min(kind, 1)],
                    device_id=(where, across[j]), device_id_type=MESH,
                ).start()
    frecv[0, col] = fsend[0]
    for c in sent:
        c.wait_send()
    fcopies = []
    for i, ref in ((0, frecv.at[0, 0:7]), (1, frecv.at[1:3])):
        fcopies.append(pltpu.make_async_remote_copy(
            src_ref=ref, dst_ref=ref, send_sem=fsem.at[i], recv_sem=fsem.at[2 + i], device_id=(sp, across[1]), device_id_type=MESH,
        ))
    for c in fcopies:
        c.wait_recv()
    summed = jnp.zeros((8, 128), F32)
    for kind in range(3):
        for j in range(8):
            summed = summed + frecv[kind, j]
    out_ref[...] = summed[0:4, :]

    assert len(names) <= NSEM
    for c in fcopies:
        c.wait_send()


def shards(env_desc, alpha, atom_desc, desc_grad, species, neighbors):
    vm = pl.BlockSpec(memory_space=pltpu.VMEM)
    V = pltpu.VMEM
    out = pl.pallas_call(
        kernel,
        out_shape=jax.ShapeDtypeStruct((4, 128), F32),
        in_specs=[pl.BlockSpec(memory_space=pl.ANY)] * 6,
        out_specs=vm,
        scratch_shapes=[
            V((1, 2048), F32), V((410, 128), BF), V((1, 128), jnp.int32), V((16, 128), jnp.int32),
            V((410, 2048), BF), V((4, 768, KC), BF), V((4, HI, KC), BF), V((2, 384, KC), BF), V((2, HI, KC), BF),
            V((2, LO, KC), BF), V((2, HI, KC), BF), V((4, BLK, KC), BF),
            V((4, 2 * BLK, KC), BF), V((2, ROWS, 128), F32), V((ROWS, 128), BF), V((ROWS, 128), BF),
            V((7, 528, 128), BF), V((7, 528, 128), BF),
            V((528, 128), F32), V((528, 128), BF), V((528, 128), BF), V((ROWS, 128), BF),
            V((2, 4 * BLK, 128), BF), V((LANES, 256), BF), V((2 * BLK, 256), BF),
            V((3, 410, 16, 128), BF), V((384, 2048), BF),
            V((2 * BLK, 256), F32), V((LANES, 256), F32), V((4 * BLK, 128), F32), V((4 * BLK, 128), BF), V((4 * BLK, 128), BF),
            V((3, BLK, 128), BF), V((3, BLK, 128), BF), V((BLK, 128), F32),
            V((3, 16, 128), F32), V((8, 2048), F32),
            V((3, 8, 128), F32), V((3, 8, 8, 128), F32),
            pltpu.SemaphoreType.DMA((6,)), pltpu.SemaphoreType.DMA((NSEM,)), pltpu.SemaphoreType.DMA((NSEM,)), pltpu.SemaphoreType.DMA((4,)),
        ],
        compiler_params=pltpu.CompilerParams(
            collective_id=0, has_side_effects=True, vmem_limit_bytes=58 * 2**20
        ),
    )(
        env_desc.T,
        alpha[None, :],
        atom_desc.T,
        species[None, :],
        neighbors.T,
        jnp.transpose(desc_grad, (2, 3, 1, 0)),
    )

    def outputs(both_ref, energy_ref, force_ref):
        energy_ref[...] = both_ref[3:4, :]
        force_ref[...] = both_ref[0:3, :]

    energies, forces = pl.pallas_call(
        outputs, out_shape=(jax.ShapeDtypeStruct((1, 128), F32), jax.ShapeDtypeStruct((3, 128), F32))
    )(out)
    return energies.reshape(128), forces


def solution(mesh):
    placed = (
        P("sp", "col"),
        P("sp"),
        P("sp", "col"),
        P("sp", None, None, "col"),
        P("sp"),
        P("sp", None),
    )
    return jax.shard_map(
        shards, mesh=mesh, in_specs=placed, out_specs=(P("sp"), P(None, "sp")), check_vma=False
    )
```

```python
import functools

import jax
import jax.numpy as jnp
from jax import lax
from jax.experimental import pallas as pl
from jax.experimental.pallas import tpu as pltpu
from jax.sharding import PartitionSpec as P

MESH = pl.DeviceIdType.MESH
BF = jnp.bfloat16
F32 = jnp.float32
BLK = 416
LO, HI = 288, 128
KC = 512
ROW1 = BLK + LO
ROWA, ROWS = 4 * ROW1, 4224
ROWF = ROWA + 4 * HI
ROWZ = ROWF + 2 * BLK
CHS = (176, 176, 96, 80)
OFF = (0, 1408, ROWA, ROWA + 8 * 96)
NLO, OLO, OEND, NHI, OHI, LANES = 416, 704, 992, 1024, 1152, 1280
NSEND, NRECV = 24, 60
NT = (((1,), (1,)), ((), ()))
TN = (((0,), (0,)), ((), ()))


def kernel(
    env_ref, alpha_hbm, at_hbm, spec_hbm, nb_hbm, grad_ref,
    out_ref,
    alpha_ref, at_ref, spec_ref, nb_ref, env, r1, nhi, olo, ohi, relay_lo, relay_hi, part, uw, acc, osend, orecv, rsend, rrecv, csum, ysend, yrecv, ball,
    ats, astack, arow, grads, onehot, prow, pcol, pown, psend, precv, mout, mrecv, proj, pairs, mrow, fsend, frecv,
    lsem, ssem, rsem, fsem,
):
    sp, col = lax.axis_index("sp"), lax.axis_index("col")
    core, yh, z = sp % 2, (sp // 2) % 2, sp // 4
    x, yl = col % 4, col // 4

    def dev(dx=0, fy=0, fh=0, dz=0, fc=0):
        a = 1 - yl if fy else yl
        h = 1 - yh if fh else yh
        k = 1 - core if fc else core
        return ((((z + dz + 8) % 8) * 2 + h) * 2 + k, a * 4 + (x + dx + 4) % 4)

    sends, recvs = {}, {}

    def copy(name, src, dst, where, out=None, into=None):
        i = sends.setdefault(out or name, len(sends))
        j = recvs.setdefault(into or name, len(recvs))
        return pltpu.make_async_remote_copy(
            src_ref=src, dst_ref=dst, send_sem=ssem.at[i], recv_sem=rsem.at[j],
            device_id=where, device_id_type=MESH,
        )

    def start(name, src, dst, where, out=None, into=None):
        c = copy(name, src, dst, where, out, into)
        c.start()
        return c

    def came(into, ref):
        copy(None, ref, ref, dev(fc=1), next(iter(sends)), into).wait_recv()

    def left(out, ref):
        copy(None, ref, ref, dev(fc=1), out, next(iter(recvs))).wait_send()

    def al(v, m):
        return pl.multiple_of(v, m)

    env_copy = pltpu.make_async_copy(env_ref, env, lsem.at[0])
    env_copy.start()
    small = []
    for i, (src, dst) in enumerate(((alpha_hbm, alpha_ref), (at_hbm, at_ref), (nb_hbm, nb_ref), (spec_hbm, spec_ref))):
        small.append(pltpu.make_async_copy(src, dst, lsem.at[2 + i]))
        small[-1].start()
    peers = [dev(dx=1), dev(dx=-1), dev(dx=2), dev(fy=1), dev(dx=1, fy=1), dev(dx=-1, fy=1), dev(dx=2, fy=1)]
    peers += [dev(fc=1), dev(fh=1), dev(dz=1), dev(dz=-1), dev(dz=2), dev(dz=-2)]
    across = [(col + j) % 8 for j in range(8)]
    before, after = (sp + 31) % 32, (sp + 1) % 32
    peers += [(s, c) for s in (before, after) for c in across]
    barrier = pltpu.get_barrier_semaphore()
    for p in peers:
        pl.semaphore_signal(barrier, inc=1, device_id=p, device_id_type=MESH)
    env_copy.wait()
    grad_copy = pltpu.make_async_copy(grad_ref, grads, lsem.at[1])
    grad_copy.start()
    for k in range(4):
        lanes = slice(k * KC, (k + 1) * KC)
        r1[k, 400:416, :] = jnp.zeros((16, KC), BF)
        r1[k, 0:400, :] = env[0:400, lanes]
        r1[k, 400:410, :] = env[400:410, lanes]
    pl.semaphore_wait(barrier, len(peers))

    def order(at_x):
        t = jnp.where(at_x % 4 >= 2, 0, 2)
        return [t, t + 1, 2 - t, 3 - t]

    ks = order(x)
    ks_left = order(x + 3)
    first = jnp.where(x < 2, 0, 2)
    own = slice(0, BLK)
    low_rows, high_rows = slice(0, LO), slice(LO, BLK)
    ys, yh_parts, os, rs = [], [], [], []
    for i in range(4):
        ys.append(start(f"y{i}", r1.at[ks[i], low_rows, :], part.at[ks[i], low_rows, :], dev(fy=1), "y"))
        start(f"n{i}", r1.at[ks_left[i], low_rows, :], r1.at[ks_left[i], NLO : NLO + LO, :], dev(dx=-1), "n")
        if i < 2:
            os.append(start(f"o{i}", r1.at[first + i, low_rows, :], relay_lo.at[i], dev(dx=1), "o"))
    for i in range(4):
        yh_parts.append(start(f"yh{i}", r1.at[ks[i], high_rows, :], part.at[ks[i], high_rows, :], dev(fy=1), "y"))
        start(f"nh{i}", r1.at[ks_left[i], high_rows, :], nhi.at[ks_left[i]], dev(dx=-1), "n")

    def n_wait(i):
        copy(f"n{i}", r1.at[ks[i], low_rows, :], r1.at[ks[i], NLO : NLO + LO, :], dev(dx=-1), "n").wait_recv()

    def nh_wait(i):
        copy(f"nh{i}", r1.at[ks[i], high_rows, :], nhi.at[ks[i]], dev(dx=-1), "n").wait_recv()

    def pass_on(i):
        os[i].wait_recv()
        if i < 2:
            rs.append(start(f"r{i}", relay_lo.at[i], olo.at[i, 64 : 64 + LO, :], dev(dx=1), "r"))
        else:
            rs.append(start(f"r{i}", relay_hi.at[i - 2], ohi.at[i - 2], dev(dx=1), "r"))

    def o_high(i):
        os.append(start(f"o{i}", r1.at[first + i - 2, high_rows, :], relay_hi.at[i - 2], dev(dx=1), "o"))

    for k in range(4):
        r1[k, OLO:768, :] = jnp.zeros((768 - OLO, KC), BF)
    for k in range(2):
        olo[k, 0:64, :] = jnp.zeros((64, KC), BF)
        olo[k, 64 + LO : 384, :] = jnp.zeros((320 - LO, KC), BF)
    for c in small:
        c.wait()
    for k in range(4):
        uw[k, own, :] = (r1[k, own, :].astype(F32) * alpha_ref[:, k * KC : (k + 1) * KC]).astype(BF)
    slots = lax.broadcasted_iota(jnp.int32, (384, 128), 0)
    for n in range(16):
        onehot[:, n * 128 : (n + 1) * 128] = jnp.where(slots == nb_ref[n : n + 1, :], 1.0, 0.0).astype(BF)
    mrow[...] = jnp.zeros_like(mrow)
    prow[...] = jnp.zeros_like(prow)
    pcol[...] = jnp.zeros_like(pcol)
    for c in (0, 1):
        acc[c, ROWZ:ROWS, :] = jnp.zeros((ROWS - ROWZ, 128), F32)
    ats[core, 400:416, :] = jnp.zeros((16, 128), BF)
    ats[core, 0:400, :] = at_ref[0:400, :]
    ats[core, 400:410, :] = at_ref[400:410, :]

    filled = set()

    def add(c, row, v):
        at = slice(row, row + v.shape[0])
        acc[c, at, :] = acc[c, at, :] + v if (c, row) in filled else v
        filled.add((c, row))

    def weigh(rows, k):
        at = slice(BLK + rows.start, BLK + rows.stop)
        weight = alpha_ref[:, pl.ds(al(k * KC, KC), KC)]
        uw[k, at, :] = (part[k, rows, :].astype(F32) * weight).astype(BF)

    def product(rows, rhs, r0, n, steps):
        v = None
        for k, rk in steps:
            d = lax.dot_general(uw[k, rows, :], rhs[rk, r0 : r0 + n, :], NT, preferred_element_type=F32)
            v = d if v is None else v + d
        return v

    def panels(v, t, base, stride):
        for j in range(v.shape[1] // 128):
            add((t + j) // 4, base + (t + j) % 4 * stride, v[:, j * 128 : (j + 1) * 128])

    front, back, every = slice(0, ROW1), slice(ROW1, 2 * BLK), slice(0, 2 * BLK)

    def low_step(i):
        ys[i].wait_recv()
        n_wait(i)
        weigh(low_rows, ks[i])
        for t in (0, 2, 4):
            panels(product(front, r1, t * 128, 256, ((ks[i], ks[i]),)), t, 0, ROW1)

    def low_opposite(j):
        rs[j].wait_recv()
        panels(product(front, olo, 0, 384, ((ks[j], j),)), 5, 0, ROW1)

    def high_step(i):
        yh_parts[i].wait_recv()
        nh_wait(i)
        weigh(high_rows, ks[i])
        steps = ((ks[i], ks[i]),)
        for t in (0, 2, 4):
            panels(product(back, r1, t * 128, 256, steps), t, ROWA, HI)
        if i < 2:
            panels(product(back, olo, 0, 384, ((ks[i], i),)), 5, ROWA, HI)
        add(0, ROWF, product(every, nhi, 0, HI, steps))

    def high_opposite(j):
        rs[2 + j].wait_recv()
        add(1, ROWF, product(every, ohi, 0, HI, ((ks[j], j),)))

    cores = {}

    def core_send(g, first, last):
        rows = slice(first, last)
        osend[rows, :] = acc[1 - core, rows, :].astype(BF)
        cores[g] = start(f"core{g}", osend.at[rows, :], orecv.at[rows, :], dev(fc=1))

    def chunk(g, d):
        return pl.ds(al(OFF[g] + ((d + 8) % 8) * CHS[g], 16), CHS[g])

    def slot(g):
        return slice(OFF[g] // 8, OFF[g] // 8 + CHS[g])

    def local(g, d):
        return acc[core, chunk(g, d), :] + orecv[chunk(g, d), :].astype(F32)

    def side(g):
        return 1 if g % 2 == 0 else -1

    routes = ((-4, -2), (-3, -1), (3, 1), (-1, -1), (1, 1), (-2, -2), (2, 2))

    def rs_copy(g, i):
        into = f"s{g}a" if i < 2 else f"s{g}b" if i == 2 else f"s{g}c"
        return copy(None, rsend.at[i, slot(g), :], rrecv.at[i, slot(g), :], dev(dz=side(g) * routes[i][1]), f"s{g}", into)

    def rs_first(g):
        if g in cores:
            cores[g].wait_recv()
        for i in (1, 0, 2):
            rsend[i, slot(g), :] = local(g, z + side(g) * routes[i][0]).astype(BF)
            rs_copy(g, i).start()

    def rs_direct(g):
        for i in (3, 4):
            rsend[i, slot(g), :] = local(g, z + side(g) * routes[i][0]).astype(BF)
            rs_copy(g, i).start()

    def rs_next(g):
        for i, arrived in ((5, (0, 1)), (6, (2,))):
            v = local(g, z + side(g) * routes[i][0])
            came(f"s{g}a" if i == 5 else f"s{g}b", rrecv.at[slice(0, 2) if i == 5 else slice(2, 3), slot(g), :])
            for j in arrived:
                v = v + rrecv[j, slot(g), :].astype(F32)
            rsend[i, slot(g), :] = v.astype(BF)
            rs_copy(g, i).start()

    def first_rows(g, d):
        return pl.ds(al(g * OFF[1] + ((d + 8) % 8) * CHS[0], 16), CHS[0])

    def first_end():
        for g in (0, 1):
            came(f"s{g}c", rrecv.at[3:7, slot(g), :])
        for g, keep in ((1 - yh, False), (yh, True)):
            rows, at = first_rows(g, z), pl.ds(al(g * CHS[0], 16), CHS[0])
            v = acc[core, rows, :] + orecv[rows, :].astype(F32)
            for j in (3, 4, 5, 6):
                v = v + rrecv[j, at, :].astype(F32)
            if keep:
                csum[0 : CHS[0], :] = v
            else:
                ysend[0 : CHS[0], :] = v.astype(BF)
                ycopies[0] = start("h0", ysend.at[0 : CHS[0], :], yrecv.at[0 : CHS[0], :], dev(fh=1))

    ycopies = {}

    def rs_end(g):
        v = local(g, z)
        came(f"s{g}c", rrecv.at[3:7, slot(g), :])
        for j in (3, 4, 5, 6):
            v = v + rrecv[j, slot(g), :].astype(F32)
        csum[slot(g), :] = v
        ysend[slot(g), :] = v.astype(BF)
        ycopies[g] = start(f"h{g}", ysend.at[slot(g), :], yrecv.at[slot(g), :], dev(fh=1))

    legs = ((0, 2), (0, -2), (0, 1), (0, -1), (-2, 2), (-2, 1), (2, -1))

    turn = 1 - 2 * core

    def ag_copy(g, i, recv=0):
        at, to = legs[i]
        into = f"g{g}{i}" if i < 2 else f"g{g}d" if g == 0 and i > 3 else f"g{g}c"
        turned_to = turn if g == 0 else side(g)
        place = z + turned_to * (at - recv * to)
        ref = ball.at[first_rows(yh, place) if g == 0 else chunk(g, place), :]
        return copy(None, ref, ref, dev(dz=turned_to * to), f"g{g}", into)

    def ag_send(g, legs_of):
        for i in legs_of:
            ag_copy(g, i).start()

    def ag_came(g, into, n):
        came(f"g{g}{into}", ball.at[OFF[g] : OFF[g] + n * CHS[g], :])

    def ag_first(g):
        ycopies[g].wait_recv()
        own_chunk = first_rows(yh, z) if g == 0 else chunk(g, z)
        ball[own_chunk, :] = (csum[slot(g), :] + yrecv[slot(g), :].astype(F32)).astype(BF)
        ag_send(g, (0, 1, 2, 3))
        if g == 0:
            over_send((7,))

    def ag_next(g):
        ag_copy(g, 0, 1).wait_recv()
        ag_send(g, (4, 5))
        ag_copy(g, 1, 1).wait_recv()
        ag_send(g, (6,))

    places = [at - to for at, to in legs] + [0]

    def over(i, where):
        ref = ball.at[first_rows(where, z + turn * places[i]), :]
        return copy("v", ref, ref, dev(fh=1))

    def over_send(own_legs, into=None):
        if into:
            ag_came(0, into, len(own_legs))
        for i in own_legs:
            over(i, yh).start()

    def over_wait():
        came("v", ball.at[0 : OFF[1], :])

    def ag_end(g):
        ag_came(g, "c", 5)

    pass_on(0)
    low_step(0)
    pass_on(1)
    o_high(2)
    o_high(3)
    low_step(1)
    low_step(2)
    low_opposite(0)
    low_step(3)
    low_opposite(1)
    core_send(0, 0, ROWA)
    pass_on(2)
    rs_first(0)
    rs_first(1)
    rs_direct(0)
    rs_direct(1)
    pass_on(3)
    high_step(0)
    high_step(1)
    rs_next(0)
    high_step(2)
    high_opposite(0)
    rs_next(1)
    high_step(3)
    high_opposite(1)
    core_send(2, ROWA, OFF[3])
    core_send(3, OFF[3], ROWS)
    own_at = ats.at[core, own, :]
    for i, where in ((1, dev(dx=-1)), (2, dev(dx=2)), (3, dev(fy=1))):
        start("a", own_at, ats.at[core, i * BLK : (i + 1) * BLK, :], where)
    rs_first(2)
    rs_first(3)
    rs_direct(2)
    rs_direct(3)
    first_end()
    rs_next(2)
    rs_next(3)
    ag_first(0)
    rs_end(2)
    rs_end(3)
    came("a", ats.at[core, BLK : 4 * BLK, :])
    hand = start("hand", ats.at[core], ats.at[core], dev(fc=1))
    ag_next(0)
    over_send((0, 1))
    over_send((2, 3), "c")
    ag_first(2)
    ag_first(3)
    over_send((4, 6, 5), "d")
    copy("hand", ats.at[1 - core], ats.at[1 - core], dev(fc=1)).wait_recv()

    def block(i, rows=own):
        return slice(i * BLK + rows.start, i * BLK + rows.stop)

    both = jnp.concatenate([ats[0], ats[1]], axis=1)
    arow[own, :] = both[block(0), :]
    arow[BLK : 2 * BLK, :] = both[block(3), :]
    astack[own, :] = both[block(0), :]
    astack[NLO:OLO, :] = both[block(1, low_rows), :]
    astack[OLO:OEND, :] = both[block(2, low_rows), :]
    astack[OEND:NHI, :] = jnp.zeros((NHI - OEND, 256), BF)
    astack[NHI:OHI, :] = both[block(1, high_rows), :]
    astack[OHI:LANES, :] = both[block(2, high_rows), :]

    def dot(a, b):
        return jnp.dot(a, b, preferred_element_type=F32)

    def turned(a, b):
        return lax.dot_general(a, b, TN, preferred_element_type=F32)

    def p_first():
        over_wait()

        @pl.when(core == 0)
        def _():
            total = jnp.zeros((BLK, 256), F32)
            for q in range(4):
                own_part = ball[q * ROW1 : q * ROW1 + BLK, :]
                partner = ball[q * ROW1 + BLK : (q + 1) * ROW1, :]
                at = slice(q * 128, (q + 1) * 128)
                total = total + dot(own_part, astack[at, :])
                terms = turned(partner, arow[BLK:ROW1, :])
                if q == 3:
                    next_only = lax.broadcasted_iota(jnp.int32, (128, 256), 0) >= BLK - 384
                    terms = terms + jnp.where(next_only, turned(own_part, arow[own, :]), 0.0)
                    prow[BLK:ROW1, :] = dot(partner, jnp.where(next_only, astack[at, :].astype(F32), 0.0).astype(BF))
                pcol[at, :] = terms
            prow[own, :] = total

        @pl.when(core == 1)
        def _():
            total = jnp.zeros((ROW1, 256), F32)
            for q in range(4):
                beta = ball[q * ROW1 : (q + 1) * ROW1, :]
                at = slice((4 + q) * 128, (5 + q) * 128)
                total = total + dot(beta, astack[at, :])
                pcol[at, :] = turned(beta, arow[front, :])
            prow[front, :] = total

    def p_second():
        ag_end(2)
        ag_end(3)
        full = ball[ROWF:ROWZ, :]

        def ends(at):
            prow[...] = prow[...] + dot(full, astack[at, :])
            pcol[at, :] = turned(full, arow[...])

        def rest(c):
            for q in range(4):
                beta = ball[ROWA + q * HI : ROWA + (q + 1) * HI, :]
                at = slice((4 * c + q) * 128, (4 * c + q + 1) * 128)
                pcol[at, :] = pcol[at, :] + turned(beta, arow[back, :])
                if c == 1:
                    prow[back, :] = prow[back, :] + dot(beta, astack[at, :])
                elif q == 3:
                    next_only = lax.broadcasted_iota(jnp.int32, (128, 256), 0) >= BLK - 384
                    a = jnp.where(next_only, astack[at, :].astype(F32), 0.0).astype(BF)
                    prow[back, :] = prow[back, :] + dot(beta, a)

        @pl.when(core == 0)
        def _():
            ends(slice(NHI, OHI))
            rest(0)

        @pl.when(core == 1)
        def _():
            ends(slice(OHI, LANES))
            rest(1)

    ag_next(2)
    ag_next(3)
    p_first()
    p_second()

    pieces = (
        (0, prow, 0, BLK), (0, pcol, 0, BLK), (BLK, pcol, NLO, LO), (BLK + LO, pcol, NHI, HI),
        (2 * BLK, pcol, OLO, LO), (2 * BLK + LO, pcol, OHI, HI), (3 * BLK, prow, BLK, BLK),
    )
    mine = pl.ds(al(core * 128, 128), 128)
    other = pl.ds(al(128 - core * 128, 128), 128)
    for lanes, keep in ((other, False), (mine, True)):
        for to, src, at, n in pieces:
            v = src[at : at + n, lanes]
            if to == 0 and src is pcol:
                v = v + prow[own, lanes]
            elif to == 0:
                continue
            if keep:
                pown[to : to + n, :] = v
            else:
                psend[to : to + n, :] = v.astype(BF)
        if not keep:
            share = start("share", psend, precv, dev(fc=1))
    share.wait_recv()
    for i, where in ((1, dev(dx=2)), (0, dev(dx=1)), (2, dev(fy=1))):
        at = slice((i + 1) * BLK, (i + 2) * BLK)
        mout[i] = (pown[at, :] + precv[at, :].astype(F32)).astype(BF)
        start("m", mout.at[i], mrecv.at[i], where)
    total = pown[own, :] + precv[own, :].astype(F32)
    came("m", mrecv)
    for i in range(3):
        total = total + mrecv[i].astype(F32)
    proj[...] = total.astype(BF).astype(F32)

    grad_copy.wait()
    zeros = [jnp.zeros((16, 128), F32) for _ in range(3)]
    energy = jnp.zeros((1, 128), F32)

    def body(step, carry):
        a0, a1, a2, e = carry
        rows = pl.ds(al(step * 16, 16), 16)
        pr = proj[rows, :]
        at = ats[core, rows, :].astype(F32)
        e = e + jnp.sum(pr * at, axis=0, keepdims=True)
        out = []
        for c, a in enumerate((a0, a1, a2)):
            for r in range(16):
                a = a + grads[c, step * 16 + r].astype(F32) * pr[r : r + 1, :]
            out.append(a)
        return (*out, e)

    a0, a1, a2, energy = lax.fori_loop(0, 25, body, (*zeros, energy))
    pr = proj[400:416, :]
    at = ats[core, 400:416, :].astype(F32)
    energy = energy + jnp.sum(pr * at, axis=0, keepdims=True)
    out = []
    for c, a in enumerate((a0, a1, a2)):
        for r in range(10):
            a = a + grads[c, 400 + r].astype(F32) * pr[r : r + 1, :]
        out.append(a)

    active = jnp.where(spec_ref[...] == 0, 1.0, 0.0)
    for c in range(3):
        pairs[c] = out[c] * active
    for n in range(16):
        mrow[0:3, n * 128 : (n + 1) * 128] = pairs[:, n, :]
    high = mrow[...].astype(BF)
    low = (mrow[...] - high.astype(F32)).astype(BF)
    spread = lax.dot_general(jnp.concatenate([high, low], axis=0), onehot[...], NT, preferred_element_type=F32)
    spread = -2.0 * (spread[0:8, :] + spread[8:16, :])
    fsend[0] = spread[:, 128:256]
    fsend[0, 0:3, :] = spread[0:3, 128:256] + 2.0 * jnp.sum(pairs[...], axis=1)
    fsend[0, 3:4, :] = energy * active
    fsend[1] = spread[:, 0:128]
    fsend[2] = spread[:, 256:384]

    for j in range(8):
        for kind, where in ((1, before), (2, after), (0, sp)):
            if j or kind:
                pltpu.make_async_remote_copy(
                    src_ref=fsend.at[kind], dst_ref=frecv.at[kind, col],
                    send_sem=fsem.at[min(kind, 1)], recv_sem=fsem.at[2 + min(kind, 1)],
                    device_id=(where, across[j]), device_id_type=MESH,
                ).start()
    frecv[0, col] = fsend[0]
    left("y", part)
    left("n", part)
    left("o", part.at[0:2])
    left("r", part.at[0:2])
    left("a", ats.at[core, BLK : 4 * BLK, :])
    left("hand", ats.at[core])
    left("share", psend)
    left("m", mout)
    left("v", ball.at[0 : OFF[1], :])
    for g in (0, 2, 3):
        cores[g].wait_send()
        ycopies[g].wait_send()
        left(f"g{g}", ball.at[OFF[g] : OFF[g] + 7 * CHS[g], :])
    for g in range(4):
        left(f"s{g}", rsend.at[:, slot(g), :])
    fcopies = []
    for i, ref in ((0, frecv.at[0, 0:7]), (1, frecv.at[1:3])):
        fcopies.append(pltpu.make_async_remote_copy(
            src_ref=ref, dst_ref=ref, send_sem=fsem.at[i], recv_sem=fsem.at[2 + i], device_id=(sp, across[1]), device_id_type=MESH,
        ))
    for c in fcopies:
        c.wait_recv()
    summed = jnp.zeros((8, 128), F32)
    for kind in range(3):
        for j in range(8):
            summed = summed + frecv[kind, j]
    out_ref[...] = summed[0:4, :]

    assert len(sends) <= NSEND and len(recvs) <= NRECV
    for c in fcopies:
        c.wait_send()


def shards(env_desc, alpha, atom_desc, desc_grad, species, neighbors):
    vm = pl.BlockSpec(memory_space=pltpu.VMEM)
    V = pltpu.VMEM
    out = pl.pallas_call(
        kernel,
        out_shape=jax.ShapeDtypeStruct((4, 128), F32),
        in_specs=[pl.BlockSpec(memory_space=pl.ANY)] * 6,
        out_specs=vm,
        scratch_shapes=[
            V((1, 2048), F32), V((410, 128), BF), V((1, 128), jnp.int32), V((16, 128), jnp.int32),
            V((410, 2048), BF), V((4, 768, KC), BF), V((4, HI, KC), BF), V((2, 384, KC), BF), V((2, HI, KC), BF),
            V((2, LO, KC), BF), V((2, HI, KC), BF), V((4, BLK, KC), BF),
            V((4, 2 * BLK, KC), BF), V((2, ROWS, 128), F32), V((ROWS, 128), BF), V((ROWS, 128), BF),
            V((7, 528, 128), BF), V((7, 528, 128), BF),
            V((528, 128), F32), V((528, 128), BF), V((528, 128), BF), V((ROWS, 128), BF),
            V((2, 4 * BLK, 128), BF), V((LANES, 256), BF), V((2 * BLK, 256), BF),
            V((3, 410, 16, 128), BF), V((384, 2048), BF),
            V((2 * BLK, 256), F32), V((LANES, 256), F32), V((4 * BLK, 128), F32), V((4 * BLK, 128), BF), V((4 * BLK, 128), BF),
            V((3, BLK, 128), BF), V((3, BLK, 128), BF), V((BLK, 128), F32),
            V((3, 16, 128), F32), V((8, 2048), F32),
            V((3, 8, 128), F32), V((3, 8, 8, 128), F32),
            pltpu.SemaphoreType.DMA((6,)), pltpu.SemaphoreType.DMA((NSEND,)), pltpu.SemaphoreType.DMA((NRECV,)), pltpu.SemaphoreType.DMA((4,)),
        ],
        compiler_params=pltpu.CompilerParams(
            collective_id=0, has_side_effects=True, vmem_limit_bytes=58 * 2**20
        ),
    )(
        env_desc.T,
        alpha[None, :],
        atom_desc.T,
        species[None, :],
        neighbors.T,
        jnp.transpose(desc_grad, (2, 3, 1, 0)),
    )

    def outputs(both_ref, energy_ref, force_ref):
        energy_ref[...] = both_ref[3:4, :]
        force_ref[...] = both_ref[0:3, :]

    energies, forces = pl.pallas_call(
        outputs, out_shape=(jax.ShapeDtypeStruct((1, 128), F32), jax.ShapeDtypeStruct((3, 128), F32))
    )(out)
    return energies.reshape(128), forces


def solution(mesh):
    placed = (
        P("sp", "col"),
        P("sp"),
        P("sp", "col"),
        P("sp", None, None, "col"),
        P("sp"),
        P("sp", None),
    )
    return jax.shard_map(
        shards, mesh=mesh, in_specs=placed, out_specs=(P("sp"), P(None, "sp")), check_vma=False
    )
```

```python
import functools

import jax
import jax.numpy as jnp
from jax import lax
from jax.experimental import pallas as pl
from jax.experimental.pallas import tpu as pltpu
from jax.sharding import PartitionSpec as P

MESH = pl.DeviceIdType.MESH
BF = jnp.bfloat16
F32 = jnp.float32
BLK = 416
LO, HI = 288, 128
KC = 512
ROW1 = BLK + LO
ROWA, ROWS = 4 * ROW1, 4224
ROWF = ROWA + 4 * HI
ROWZ = ROWF + 2 * BLK
CHS = (176, 176, 96, 80)
OFF = (0, 1408, ROWA, ROWA + 8 * 96)
NLO, OLO, OEND, NHI, OHI, LANES = 416, 704, 992, 1024, 1152, 1280
NSEND, NRECV = 24, 60
NT = (((1,), (1,)), ((), ()))
TN = (((0,), (0,)), ((), ()))


def kernel(
    env_ref, alpha_hbm, at_hbm, spec_hbm, nb_hbm, grad_ref,
    energy_ref, force_ref,
    alpha_ref, at_ref, spec_ref, nb_ref, env, r1, nhi, olo, ohi, relay_lo, relay_hi, part, uw, acc, osend, orecv, rsend, rrecv, csum, ysend, yrecv, ball,
    ats, astack, arow, grads, onehot, prow, pcol, pown, psend, precv, mout, mrecv, proj, pairs, mrow, fsend, frecv,
    lsem, ssem, rsem, fsem,
):
    sp, col = lax.axis_index("sp"), lax.axis_index("col")
    core, yh, z = sp % 2, (sp // 2) % 2, sp // 4
    x, yl = col % 4, col // 4

    def dev(dx=0, fy=0, fh=0, dz=0, fc=0):
        a = 1 - yl if fy else yl
        h = 1 - yh if fh else yh
        k = 1 - core if fc else core
        return ((((z + dz + 8) % 8) * 2 + h) * 2 + k, a * 4 + (x + dx + 4) % 4)

    sends, recvs = {}, {}

    def copy(name, src, dst, where, out=None, into=None):
        i = sends.setdefault(out or name, len(sends))
        j = recvs.setdefault(into or name, len(recvs))
        return pltpu.make_async_remote_copy(
            src_ref=src, dst_ref=dst, send_sem=ssem.at[i], recv_sem=rsem.at[j],
            device_id=where, device_id_type=MESH,
        )

    def start(name, src, dst, where, out=None, into=None):
        c = copy(name, src, dst, where, out, into)
        c.start()
        return c

    def came(into, ref):
        copy(None, ref, ref, dev(fc=1), next(iter(sends)), into).wait_recv()

    def left(out, ref):
        copy(None, ref, ref, dev(fc=1), out, next(iter(recvs))).wait_send()

    def al(v, m):
        return pl.multiple_of(v, m)

    env_copy = pltpu.make_async_copy(env_ref, env, lsem.at[0])
    env_copy.start()
    small = []
    for i, (src, dst) in enumerate(((alpha_hbm, alpha_ref), (at_hbm, at_ref), (nb_hbm, nb_ref), (spec_hbm, spec_ref))):
        small.append(pltpu.make_async_copy(src, dst, lsem.at[2 + i]))
        small[-1].start()
    peers = [dev(dx=1), dev(dx=-1), dev(dx=2), dev(fy=1), dev(dx=1, fy=1), dev(dx=-1, fy=1), dev(dx=2, fy=1)]
    peers += [dev(fc=1), dev(fh=1), dev(dz=1), dev(dz=-1), dev(dz=2), dev(dz=-2)]
    across = [(col + j) % 8 for j in range(8)]
    before, after = (sp + 31) % 32, (sp + 1) % 32
    peers += [(s, c) for s in (before, after) for c in across]
    barrier = pltpu.get_barrier_semaphore()
    for p in peers:
        pl.semaphore_signal(barrier, inc=1, device_id=p, device_id_type=MESH)
    env_copy.wait()
    grad_copy = pltpu.make_async_copy(grad_ref, grads, lsem.at[1])
    grad_copy.start()
    for k in range(4):
        lanes = slice(k * KC, (k + 1) * KC)
        r1[k, 400:416, :] = jnp.zeros((16, KC), BF)
        r1[k, 0:400, :] = env[0:400, lanes]
        r1[k, 400:410, :] = env[400:410, lanes]
    pl.semaphore_wait(barrier, len(peers))

    def order(at_x):
        t = jnp.where(at_x % 4 >= 2, 0, 2)
        return [t, t + 1, 2 - t, 3 - t]

    ks = order(x)
    ks_left = order(x + 3)
    first = jnp.where(x < 2, 0, 2)
    own = slice(0, BLK)
    low_rows, high_rows = slice(0, LO), slice(LO, BLK)
    ys, yh_parts, os, rs = [], [], [], []
    for i in range(4):
        ys.append(start(f"y{i}", r1.at[ks[i], low_rows, :], part.at[ks[i], low_rows, :], dev(fy=1), "y"))
        start(f"n{i}", r1.at[ks_left[i], low_rows, :], r1.at[ks_left[i], NLO : NLO + LO, :], dev(dx=-1), "n")
        if i < 2:
            os.append(start(f"o{i}", r1.at[first + i, low_rows, :], relay_lo.at[i], dev(dx=1), "o"))
    for i in range(4):
        yh_parts.append(start(f"yh{i}", r1.at[ks[i], high_rows, :], part.at[ks[i], high_rows, :], dev(fy=1), "y"))
        start(f"nh{i}", r1.at[ks_left[i], high_rows, :], nhi.at[ks_left[i]], dev(dx=-1), "n")

    def n_wait(i):
        copy(f"n{i}", r1.at[ks[i], low_rows, :], r1.at[ks[i], NLO : NLO + LO, :], dev(dx=-1), "n").wait_recv()

    def nh_wait(i):
        copy(f"nh{i}", r1.at[ks[i], high_rows, :], nhi.at[ks[i]], dev(dx=-1), "n").wait_recv()

    def pass_on(i):
        os[i].wait_recv()
        if i < 2:
            rs.append(start(f"r{i}", relay_lo.at[i], olo.at[i, 64 : 64 + LO, :], dev(dx=1), "r"))
        else:
            rs.append(start(f"r{i}", relay_hi.at[i - 2], ohi.at[i - 2], dev(dx=1), "r"))

    def o_high(i):
        os.append(start(f"o{i}", r1.at[first + i - 2, high_rows, :], relay_hi.at[i - 2], dev(dx=1), "o"))

    for k in range(4):
        r1[k, OLO:768, :] = jnp.zeros((768 - OLO, KC), BF)
    for k in range(2):
        olo[k, 0:64, :] = jnp.zeros((64, KC), BF)
        olo[k, 64 + LO : 384, :] = jnp.zeros((320 - LO, KC), BF)
    for c in small:
        c.wait()
    for k in range(4):
        uw[k, own, :] = (r1[k, own, :].astype(F32) * alpha_ref[:, k * KC : (k + 1) * KC]).astype(BF)
    slots = lax.broadcasted_iota(jnp.int32, (384, 128), 0)
    for n in range(16):
        onehot[:, n * 128 : (n + 1) * 128] = jnp.where(slots == nb_ref[n : n + 1, :], 1.0, 0.0).astype(BF)
    mrow[...] = jnp.zeros_like(mrow)
    prow[...] = jnp.zeros_like(prow)
    pcol[...] = jnp.zeros_like(pcol)
    for c in (0, 1):
        acc[c, ROWZ:ROWS, :] = jnp.zeros((ROWS - ROWZ, 128), F32)
    ats[core, 400:416, :] = jnp.zeros((16, 128), BF)
    ats[core, 0:400, :] = at_ref[0:400, :]
    ats[core, 400:410, :] = at_ref[400:410, :]

    filled = set()

    def add(c, row, v):
        at = slice(row, row + v.shape[0])
        acc[c, at, :] = acc[c, at, :] + v if (c, row) in filled else v
        filled.add((c, row))

    def weigh(rows, k):
        at = slice(BLK + rows.start, BLK + rows.stop)
        weight = alpha_ref[:, pl.ds(al(k * KC, KC), KC)]
        uw[k, at, :] = (part[k, rows, :].astype(F32) * weight).astype(BF)

    def product(rows, rhs, r0, n, steps):
        v = None
        for k, rk in steps:
            d = lax.dot_general(uw[k, rows, :], rhs[rk, r0 : r0 + n, :], NT, preferred_element_type=F32)
            v = d if v is None else v + d
        return v

    def panels(v, t, base, stride):
        for j in range(v.shape[1] // 128):
            add((t + j) // 4, base + (t + j) % 4 * stride, v[:, j * 128 : (j + 1) * 128])

    front, back, every = slice(0, ROW1), slice(ROW1, 2 * BLK), slice(0, 2 * BLK)

    def low_step(i):
        ys[i].wait_recv()
        n_wait(i)
        weigh(low_rows, ks[i])
        for t in (0, 2, 4):
            panels(product(front, r1, t * 128, 256, ((ks[i], ks[i]),)), t, 0, ROW1)

    def low_opposite(j):
        rs[j].wait_recv()
        panels(product(front, olo, 0, 384, ((ks[j], j),)), 5, 0, ROW1)

    def high_step(i):
        yh_parts[i].wait_recv()
        nh_wait(i)
        weigh(high_rows, ks[i])
        steps = ((ks[i], ks[i]),)
        for t in (0, 2, 4):
            panels(product(back, r1, t * 128, 256, steps), t, ROWA, HI)
        if i < 2:
            panels(product(back, olo, 0, 384, ((ks[i], i),)), 5, ROWA, HI)
        add(0, ROWF, product(every, nhi, 0, HI, steps))

    def high_opposite(j):
        rs[2 + j].wait_recv()
        add(1, ROWF, product(every, ohi, 0, HI, ((ks[j], j),)))

    cores = {}

    def core_send(g, first, last):
        rows = slice(first, last)
        osend[rows, :] = acc[1 - core, rows, :].astype(BF)
        cores[g] = start(f"core{g}", osend.at[rows, :], orecv.at[rows, :], dev(fc=1))

    def chunk(g, d):
        return pl.ds(al(OFF[g] + ((d + 8) % 8) * CHS[g], 16), CHS[g])

    def slot(g):
        return slice(OFF[g] // 8, OFF[g] // 8 + CHS[g])

    def local(g, d):
        return acc[core, chunk(g, d), :] + orecv[chunk(g, d), :].astype(F32)

    def side(g):
        return 1 if g % 2 == 0 else -1

    routes = ((-4, -2), (-3, -1), (3, 1), (-1, -1), (1, 1), (-2, -2), (2, 2))

    def rs_copy(g, i):
        into = f"s{g}a" if i < 2 else f"s{g}b" if i == 2 else f"s{g}c"
        return copy(None, rsend.at[i, slot(g), :], rrecv.at[i, slot(g), :], dev(dz=side(g) * routes[i][1]), f"s{g}", into)

    def rs_first(g):
        if g in cores:
            cores[g].wait_recv()
        for i in (1, 0, 2):
            rsend[i, slot(g), :] = local(g, z + side(g) * routes[i][0]).astype(BF)
            rs_copy(g, i).start()

    def rs_direct(g):
        for i in (3, 4):
            rsend[i, slot(g), :] = local(g, z + side(g) * routes[i][0]).astype(BF)
            rs_copy(g, i).start()

    def rs_next(g):
        for i, arrived in ((5, (0, 1)), (6, (2,))):
            v = local(g, z + side(g) * routes[i][0])
            came(f"s{g}a" if i == 5 else f"s{g}b", rrecv.at[slice(0, 2) if i == 5 else slice(2, 3), slot(g), :])
            for j in arrived:
                v = v + rrecv[j, slot(g), :].astype(F32)
            rsend[i, slot(g), :] = v.astype(BF)
            rs_copy(g, i).start()

    def first_rows(g, d):
        return pl.ds(al(g * OFF[1] + ((d + 8) % 8) * CHS[0], 16), CHS[0])

    def first_end():
        for g in (0, 1):
            came(f"s{g}c", rrecv.at[3:7, slot(g), :])
        for g, keep in ((1 - yh, False), (yh, True)):
            rows, at = first_rows(g, z), pl.ds(al(g * CHS[0], 16), CHS[0])
            v = acc[core, rows, :] + orecv[rows, :].astype(F32)
            for j in (3, 4, 5, 6):
                v = v + rrecv[j, at, :].astype(F32)
            if keep:
                csum[0 : CHS[0], :] = v
            else:
                ysend[0 : CHS[0], :] = v.astype(BF)
                ycopies[0] = start("h0", ysend.at[0 : CHS[0], :], yrecv.at[0 : CHS[0], :], dev(fh=1))

    ycopies = {}

    def rs_end(g):
        v = local(g, z)
        came(f"s{g}c", rrecv.at[3:7, slot(g), :])
        for j in (3, 4, 5, 6):
            v = v + rrecv[j, slot(g), :].astype(F32)
        csum[slot(g), :] = v
        ysend[slot(g), :] = v.astype(BF)
        ycopies[g] = start(f"h{g}", ysend.at[slot(g), :], yrecv.at[slot(g), :], dev(fh=1))

    legs = ((0, 2), (0, -2), (0, 1), (0, -1), (-2, 2), (-2, 1), (2, -1))

    turn = 1 - 2 * core

    def ag_copy(g, i, recv=0):
        at, to = legs[i]
        into = f"g{g}{i}" if i < 2 else f"g{g}d" if g == 0 and i > 3 else f"g{g}c"
        turned_to = turn if g == 0 else side(g)
        place = z + turned_to * (at - recv * to)
        ref = ball.at[first_rows(yh, place) if g == 0 else chunk(g, place), :]
        return copy(None, ref, ref, dev(dz=turned_to * to), f"g{g}", into)

    def ag_send(g, legs_of):
        for i in legs_of:
            ag_copy(g, i).start()

    def ag_came(g, into, n):
        came(f"g{g}{into}", ball.at[OFF[g] : OFF[g] + n * CHS[g], :])

    def ag_first(g):
        ycopies[g].wait_recv()
        own_chunk = first_rows(yh, z) if g == 0 else chunk(g, z)
        ball[own_chunk, :] = (csum[slot(g), :] + yrecv[slot(g), :].astype(F32)).astype(BF)
        ag_send(g, (0, 1) if g else (0, 1, 2, 3))
        if g == 0:
            over_send((7,))

    def ag_next(g):
        ag_copy(g, 0, 1).wait_recv()
        ag_send(g, (4, 5))
        ag_copy(g, 1, 1).wait_recv()
        ag_send(g, (6,))

    places = [at - to for at, to in legs] + [0]

    def over(i, where):
        ref = ball.at[first_rows(where, z + turn * places[i]), :]
        return copy("v", ref, ref, dev(fh=1))

    def over_send(own_legs, into=None):
        if into:
            ag_came(0, into, len(own_legs))
        for i in own_legs:
            over(i, yh).start()

    def over_wait():
        came("v", ball.at[0 : OFF[1], :])

    def ag_end(g):
        ag_came(g, "c", 5)

    pass_on(0)
    low_step(0)
    pass_on(1)
    o_high(2)
    o_high(3)
    low_step(1)
    low_step(2)
    low_opposite(0)
    low_step(3)
    low_opposite(1)
    core_send(0, 0, ROWA)
    pass_on(2)
    rs_first(0)
    rs_first(1)
    rs_direct(0)
    rs_direct(1)
    pass_on(3)
    high_step(0)
    high_step(1)
    rs_next(0)
    high_step(2)
    high_opposite(0)
    rs_next(1)
    high_step(3)
    high_opposite(1)
    core_send(2, ROWA, OFF[3])
    core_send(3, OFF[3], ROWS)
    own_at = ats.at[core, own, :]
    for i, where in ((1, dev(dx=-1)), (2, dev(dx=2)), (3, dev(fy=1))):
        start("a", own_at, ats.at[core, i * BLK : (i + 1) * BLK, :], where)
    rs_first(2)
    rs_first(3)
    rs_direct(2)
    rs_direct(3)
    first_end()
    rs_next(2)
    rs_next(3)
    ag_first(0)
    rs_end(2)
    rs_end(3)
    came("a", ats.at[core, BLK : 4 * BLK, :])
    hand = start("hand", ats.at[core], ats.at[core], dev(fc=1))
    ag_next(0)
    over_send((0, 1))
    over_send((2, 3), "c")
    ag_first(2)
    ag_first(3)
    ag_send(2, (2, 3))
    ag_send(3, (2, 3))
    over_send((4, 6, 5), "d")
    copy("hand", ats.at[1 - core], ats.at[1 - core], dev(fc=1)).wait_recv()

    def block(i, rows=own):
        return slice(i * BLK + rows.start, i * BLK + rows.stop)

    both = jnp.concatenate([ats[0], ats[1]], axis=1)
    arow[own, :] = both[block(0), :]
    arow[BLK : 2 * BLK, :] = both[block(3), :]
    astack[own, :] = both[block(0), :]
    astack[NLO:OLO, :] = both[block(1, low_rows), :]
    astack[OLO:OEND, :] = both[block(2, low_rows), :]
    astack[OEND:NHI, :] = jnp.zeros((NHI - OEND, 256), BF)
    astack[NHI:OHI, :] = both[block(1, high_rows), :]
    astack[OHI:LANES, :] = both[block(2, high_rows), :]

    def dot(a, b):
        return jnp.dot(a, b, preferred_element_type=F32)

    def turned(a, b):
        return lax.dot_general(a, b, TN, preferred_element_type=F32)

    def p_first():
        over_wait()

        @pl.when(core == 0)
        def _():
            total = jnp.zeros((BLK, 256), F32)
            for q in range(4):
                own_part = ball[q * ROW1 : q * ROW1 + BLK, :]
                partner = ball[q * ROW1 + BLK : (q + 1) * ROW1, :]
                at = slice(q * 128, (q + 1) * 128)
                total = total + dot(own_part, astack[at, :])
                terms = turned(partner, arow[BLK:ROW1, :])
                if q == 3:
                    next_only = lax.broadcasted_iota(jnp.int32, (128, 256), 0) >= BLK - 384
                    terms = terms + jnp.where(next_only, turned(own_part, arow[own, :]), 0.0)
                    prow[BLK:ROW1, :] = dot(partner, jnp.where(next_only, astack[at, :].astype(F32), 0.0).astype(BF))
                pcol[at, :] = terms
            prow[own, :] = total

        @pl.when(core == 1)
        def _():
            total = jnp.zeros((ROW1, 256), F32)
            for q in range(4):
                beta = ball[q * ROW1 : (q + 1) * ROW1, :]
                at = slice((4 + q) * 128, (5 + q) * 128)
                total = total + dot(beta, astack[at, :])
                pcol[at, :] = turned(beta, arow[front, :])
            prow[front, :] = total

    def p_second():
        ag_end(2)
        ag_end(3)
        full = ball[ROWF:ROWZ, :]

        def ends(at):
            prow[...] = prow[...] + dot(full, astack[at, :])
            pcol[at, :] = turned(full, arow[...])

        def rest(c):
            for q in range(4):
                beta = ball[ROWA + q * HI : ROWA + (q + 1) * HI, :]
                at = slice((4 * c + q) * 128, (4 * c + q + 1) * 128)
                pcol[at, :] = pcol[at, :] + turned(beta, arow[back, :])
                if c == 1:
                    prow[back, :] = prow[back, :] + dot(beta, astack[at, :])
                elif q == 3:
                    next_only = lax.broadcasted_iota(jnp.int32, (128, 256), 0) >= BLK - 384
                    a = jnp.where(next_only, astack[at, :].astype(F32), 0.0).astype(BF)
                    prow[back, :] = prow[back, :] + dot(beta, a)

        @pl.when(core == 0)
        def _():
            ends(slice(NHI, OHI))
            rest(0)

        @pl.when(core == 1)
        def _():
            ends(slice(OHI, LANES))
            rest(1)

    ag_next(2)
    ag_next(3)
    p_first()
    p_second()

    pieces = (
        (0, prow, 0, BLK), (0, pcol, 0, BLK), (BLK, pcol, NLO, LO), (BLK + LO, pcol, NHI, HI),
        (2 * BLK, pcol, OLO, LO), (2 * BLK + LO, pcol, OHI, HI), (3 * BLK, prow, BLK, BLK),
    )
    mine = pl.ds(al(core * 128, 128), 128)
    other = pl.ds(al(128 - core * 128, 128), 128)
    for lanes, keep in ((other, False), (mine, True)):
        for to, src, at, n in pieces:
            v = src[at : at + n, lanes]
            if to == 0 and src is pcol:
                v = v + prow[own, lanes]
            elif to == 0:
                continue
            if keep:
                pown[to : to + n, :] = v
            else:
                psend[to : to + n, :] = v.astype(BF)
        if not keep:
            share = start("share", psend, precv, dev(fc=1))
    share.wait_recv()
    for i, where in ((1, dev(dx=2)), (0, dev(dx=1)), (2, dev(fy=1))):
        at = slice((i + 1) * BLK, (i + 2) * BLK)
        mout[i] = (pown[at, :] + precv[at, :].astype(F32)).astype(BF)
        start("m", mout.at[i], mrecv.at[i], where)
    total = pown[own, :] + precv[own, :].astype(F32)
    came("m", mrecv)
    for i in range(3):
        total = total + mrecv[i].astype(F32)
    proj[...] = total.astype(BF).astype(F32)

    grad_copy.wait()
    zeros = [jnp.zeros((16, 128), F32) for _ in range(3)]
    energy = jnp.zeros((1, 128), F32)

    def body(step, carry):
        a0, a1, a2, e = carry
        rows = pl.ds(al(step * 16, 16), 16)
        pr = proj[rows, :]
        at = ats[core, rows, :].astype(F32)
        e = e + jnp.sum(pr * at, axis=0, keepdims=True)
        out = []
        for c, a in enumerate((a0, a1, a2)):
            for r in range(16):
                a = a + grads[c, step * 16 + r].astype(F32) * pr[r : r + 1, :]
            out.append(a)
        return (*out, e)

    a0, a1, a2, energy = lax.fori_loop(0, 25, body, (*zeros, energy))
    pr = proj[400:416, :]
    at = ats[core, 400:416, :].astype(F32)
    energy = energy + jnp.sum(pr * at, axis=0, keepdims=True)
    out = []
    for c, a in enumerate((a0, a1, a2)):
        for r in range(10):
            a = a + grads[c, 400 + r].astype(F32) * pr[r : r + 1, :]
        out.append(a)

    active = jnp.where(spec_ref[...] == 0, 1.0, 0.0)
    for c in range(3):
        pairs[c] = out[c] * active
    for n in range(16):
        mrow[0:3, n * 128 : (n + 1) * 128] = pairs[:, n, :]
    high = mrow[...].astype(BF)
    low = (mrow[...] - high.astype(F32)).astype(BF)
    spread = lax.dot_general(jnp.concatenate([high, low], axis=0), onehot[...], NT, preferred_element_type=F32)
    spread = -2.0 * (spread[0:8, :] + spread[8:16, :])
    fsend[0] = spread[:, 128:256]
    fsend[0, 0:3, :] = spread[0:3, 128:256] + 2.0 * jnp.sum(pairs[...], axis=1)
    fsend[0, 3:4, :] = energy * active
    fsend[1] = spread[:, 0:128]
    fsend[2] = spread[:, 256:384]

    for kind, where in ((1, before), (2, after), (0, sp)):
        for j in (2, 6, 4, 3, 5, 1, 7, 0):
            if j or kind:
                pltpu.make_async_remote_copy(
                    src_ref=fsend.at[kind], dst_ref=frecv.at[kind, col],
                    send_sem=fsem.at[min(kind, 1)], recv_sem=fsem.at[2 + min(kind, 1)],
                    device_id=(where, across[j]), device_id_type=MESH,
                ).start()
    frecv[0, col] = fsend[0]
    left("y", part)
    left("n", part)
    left("o", part.at[0:2])
    left("r", part.at[0:2])
    left("a", ats.at[core, BLK : 4 * BLK, :])
    left("hand", ats.at[core])
    left("share", psend)
    left("m", mout)
    left("v", ball.at[0 : OFF[1], :])
    for g in (0, 2, 3):
        cores[g].wait_send()
        ycopies[g].wait_send()
        left(f"g{g}", ball.at[OFF[g] : OFF[g] + 7 * CHS[g], :])
    for g in range(4):
        left(f"s{g}", rsend.at[:, slot(g), :])
    fcopies = []
    for i, ref in ((0, frecv.at[0, 0:7]), (1, frecv.at[1:3])):
        fcopies.append(pltpu.make_async_remote_copy(
            src_ref=ref, dst_ref=ref, send_sem=fsem.at[i], recv_sem=fsem.at[2 + i], device_id=(sp, across[1]), device_id_type=MESH,
        ))
    for c in fcopies:
        c.wait_recv()
    summed = jnp.zeros((8, 128), F32)
    for kind in range(3):
        for j in range(8):
            summed = summed + frecv[kind, j]
    energy_ref[...] = summed[3:4, :]
    force_ref[...] = summed[0:3, :]

    assert len(sends) <= NSEND and len(recvs) <= NRECV
    for c in fcopies:
        c.wait_send()


def shards(env_desc, alpha, atom_desc, desc_grad, species, neighbors):
    vm = pl.BlockSpec(memory_space=pltpu.VMEM)
    V = pltpu.VMEM
    held = pl.pallas_call(
        kernel,
        out_shape=(jax.ShapeDtypeStruct((1, 128), F32), jax.ShapeDtypeStruct((3, 128), F32)),
        in_specs=[pl.BlockSpec(memory_space=pl.ANY)] * 6,
        out_specs=(vm, vm),
        scratch_shapes=[
            V((1, 2048), F32), V((410, 128), BF), V((1, 128), jnp.int32), V((16, 128), jnp.int32),
            V((410, 2048), BF), V((4, 768, KC), BF), V((4, HI, KC), BF), V((2, 384, KC), BF), V((2, HI, KC), BF),
            V((2, LO, KC), BF), V((2, HI, KC), BF), V((4, BLK, KC), BF),
            V((4, 2 * BLK, KC), BF), V((2, ROWS, 128), F32), V((ROWS, 128), BF), V((ROWS, 128), BF),
            V((7, 528, 128), BF), V((7, 528, 128), BF),
            V((528, 128), F32), V((528, 128), BF), V((528, 128), BF), V((ROWS, 128), BF),
            V((2, 4 * BLK, 128), BF), V((LANES, 256), BF), V((2 * BLK, 256), BF),
            V((3, 410, 16, 128), BF), V((384, 2048), BF),
            V((2 * BLK, 256), F32), V((LANES, 256), F32), V((4 * BLK, 128), F32), V((4 * BLK, 128), BF), V((4 * BLK, 128), BF),
            V((3, BLK, 128), BF), V((3, BLK, 128), BF), V((BLK, 128), F32),
            V((3, 16, 128), F32), V((8, 2048), F32),
            V((3, 8, 128), F32), V((3, 8, 8, 128), F32),
            pltpu.SemaphoreType.DMA((6,)), pltpu.SemaphoreType.DMA((NSEND,)), pltpu.SemaphoreType.DMA((NRECV,)), pltpu.SemaphoreType.DMA((4,)),
        ],
        compiler_params=pltpu.CompilerParams(
            collective_id=0, has_side_effects=True, vmem_limit_bytes=58 * 2**20
        ),
    )(
        env_desc.T,
        alpha[None, :],
        atom_desc.T,
        species[None, :],
        neighbors.T,
        jnp.transpose(desc_grad, (2, 3, 1, 0)),
    )

    def outputs(energy_ref, force_ref, energy_out, force_out, sem):
        copies = [
            pltpu.make_async_copy(energy_ref, energy_out, sem.at[0]),
            pltpu.make_async_copy(force_ref, force_out, sem.at[1]),
        ]
        for c in copies:
            c.start()
        for c in copies:
            c.wait()

    anywhere = pl.BlockSpec(memory_space=pl.ANY)
    energies, forces = pl.pallas_call(
        outputs,
        out_shape=(jax.ShapeDtypeStruct((1, 128), F32), jax.ShapeDtypeStruct((3, 128), F32)),
        in_specs=[anywhere, anywhere],
        out_specs=(anywhere, anywhere),
        scratch_shapes=[pltpu.SemaphoreType.DMA((2,))],
    )(*held)
    return energies.reshape(128), forces


def solution(mesh):
    placed = (
        P("sp", "col"),
        P("sp"),
        P("sp", "col"),
        P("sp", None, None, "col"),
        P("sp"),
        P("sp", None),
    )
    return jax.shard_map(
        shards, mesh=mesh, in_specs=placed, out_specs=(P("sp"), P(None, "sp")), check_vma=False
    )
```
